32 devices in a mesh: member: 4 (over y, core), lat: 2 (over x), lon: 4 (over z).
Axes of the slice: x: 2, y: 2, z: 4, core: 2. Of those that a mesh axis runs over, the one named last changes fastest.
Arguments:
- fields: bfloat16 [12, 32, 32, 256], P('member', 'lat', 'lon'), may hold values from -6 to 6
- land_mask: int32 [32, 32], P('lat', 'lon'), may hold values 0 or 1
- offsets: int32 [2], replicated, may hold values from 1 to 7
- land_embed: float32 [256], replicated, may hold values from -5 to 5
- win_qkv: bfloat16 [256, 768], replicated, may hold values from -16 to 16, as said below
- win_out: bfloat16 [256, 256], replicated, may hold values from -0.375 to 0.375
- win_up: bfloat16 [256, 1024], replicated, may hold values from -0.375 to 0.375
- win_down: bfloat16 [1024, 256], replicated, may hold values from -0.1875 to 0.1875
- mem_qkv: bfloat16 [256, 768], replicated, may hold values from -16 to 16, as said below
- mem_out: bfloat16 [256, 256], replicated, may hold values from -0.375 to 0.375
- shift_qkv: bfloat16 [256, 768], replicated, may hold values from -16 to 16, as said below
- shift_out: bfloat16 [256, 256], replicated, may hold values from -0.375 to 0.375
- shift_up: bfloat16 [256, 1024], replicated, may hold values from -0.375 to 0.375
- shift_down: bfloat16 [1024, 256], replicated, may hold values from -0.1875 to 0.1875
Outputs:
- updated: bfloat16 [12, 32, 32, 256], P('member', 'lat', 'lon')
The draws below stay inside these ranges and needn't reach their ends.
Inputs may be any that keep to these rules, and one draw needn't show every extreme that they name: `win_qkv`: query, key and value projection: columns 0 to 255 are queries, then keys, then values, each in 4 heads of 64. `mem_qkv`: laid out as win_qkv. `shift_qkv`: laid out as win_qkv.
All inputs are finite; a program needn't handle non-finite values. No bound on the sum of `land_mask` on one device may be relied on, other than what follows from the above.
Results may differ from the reference program's by a relative error of at most 0.013.
Values may be sent and summed in bfloat16 or wider, within the bound.
No kernel may reach another device: no remote copies, remote signals or barrier semaphores. Data moves between devices by JAX's collectives and lax.ppermute only.
A program may use at most 64 MiB of HBM per device.

```python
import math
import jax
import jax.numpy as jnp
from jax import lax

D = 256
HEADS = 4
HID = 1024
WIN = 8
MEMBERS = 12
NLAT = 32
NLON = 32


def attention_weights(key, salt_value):
    key = jax.random.fold_in(key, salt_value)
    base_key = jax.random.fold_in(key, 0)
    matrix = jax.random.truncated_normal(base_key, -4.0, 4.0, (D, 3 * D), jnp.float32) / math.sqrt(D)
    return matrix.astype(jnp.bfloat16)


def draw_win_qkv(key, part):
    return attention_weights(key, 11)


def draw_mem_qkv(key, part):
    return attention_weights(key, 12)


def draw_shift_qkv(key, part):
    return attention_weights(key, 13)


def place_ends(drawn, stream_key, low, top_value):
    longest = drawn.shape.index(max(drawn.shape))
    spots = []
    for shift in (0, 1):
        where = [jax.random.randint(jax.random.fold_in(stream_key, axis), (), 0, length) for axis, length in enumerate(drawn.shape)]
        where[longest] = (where[longest] + shift) % drawn.shape[longest]
        spots.append(tuple(where))
    return drawn.at[spots[0]].set(low).at[spots[1]].set(top_value)


def block_levels(stream_key, extent, cuts, low, top_value):
    def one(position, shards_of):
        draws = jax.random.uniform(jax.random.fold_in(jax.random.fold_in(stream_key, 6), position), (shards_of,), jnp.float32, low / len(cuts), top_value / len(cuts))
        return jnp.repeat(jnp.exp(draws), extent[position] // shards_of).reshape((-1,) + (1,) * (len(extent) - position - 1))

    factor_of = one(*cuts[0])
    for cut in cuts[1:]:
        factor_of = factor_of * one(*cut)
    return factor_of


def bell_draw(stream_key, extent, scale, bound, cuts=(), held_as=jnp.bfloat16):
    array = jax.random.normal(stream_key, extent, jnp.float32) * scale
    if len(cuts) > 0:
        array = block_levels(stream_key, extent, cuts, -0.22, 0.18) * array
    return jnp.clip(array, min=-bound, max=bound).astype(held_as)


def setup_inputs(seed: int = 0) -> dict:
    seeds = jax.random.split(jax.random.key(seed), 15)
    return {
        "fields": bell_draw(seeds[0], (MEMBERS, NLAT, NLON, D), 1.0, 6.0, ((0, 4), (1, 2), (2, 4))),
        "land_mask": place_ends((jax.random.randint(seeds[1], (NLAT, NLON), 0, 10) < 3).astype(jnp.int32), jax.random.fold_in(seeds[1], 1), 0, 1),
        "offsets": jax.random.randint(seeds[2], (2,), 1, WIN).astype(jnp.int32),
        "land_embed": bell_draw(seeds[3], (D,), 1.0, 5.0, (), jnp.float32),
        "win_qkv": draw_win_qkv(jax.random.fold_in(seeds[14], 71), 0),
        "win_out": bell_draw(seeds[5], (D, D), D ** -0.5, 0.375),
        "win_up": bell_draw(seeds[6], (D, HID), D ** -0.5, 0.375),
        "win_down": bell_draw(seeds[7], (HID, D), HID ** -0.5, 0.1875),
        "mem_qkv": draw_mem_qkv(jax.random.fold_in(seeds[14], 71), 0),
        "mem_out": bell_draw(seeds[9], (D, D), D ** -0.5, 0.375),
        "shift_qkv": draw_shift_qkv(jax.random.fold_in(seeds[14], 71), 0),
        "shift_out": bell_draw(seeds[11], (D, D), D ** -0.5, 0.375),
        "shift_up": bell_draw(seeds[12], (D, HID), D ** -0.5, 0.375),
        "shift_down": bell_draw(seeds[13], (HID, D), HID ** -0.5, 0.1875),
    }


epsilon = 1e-05

def normalize(stream):
    average = lax.optimization_barrier(jnp.mean(stream, axis=-1, keepdims=True))
    centered = stream - average
    spread = lax.optimization_barrier(jnp.mean(centered * centered, axis=-1, keepdims=True))
    return (centered * lax.rsqrt(spread + epsilon)).astype(jnp.bfloat16)

def project(inputs, matrix):
    flattened = inputs.reshape(-1, inputs.shape[-1])
    result = jnp.dot(flattened, matrix, preferred_element_type=jnp.float32)
    return result.reshape(inputs.shape[:-1] + (matrix.shape[1],))

def to_windows(tensor):
    height, breadth, channels = tensor.shape
    tensor = tensor.reshape(height // WIN, WIN, breadth // WIN, WIN, channels)
    return tensor.transpose(0, 2, 1, 3, 4).reshape(height // WIN, breadth // WIN, WIN * WIN, channels)

def from_windows(tensor, height, breadth):
    channels = tensor.shape[-1]
    tensor = tensor.reshape(height // WIN, breadth // WIN, WIN, WIN, channels).transpose(0, 2, 1, 3, 4)
    return tensor.reshape(height, breadth, channels)

def window_attention(qkv_rows, window_tag):
    height, breadth, triple = qkv_rows.shape
    channels = triple // 3
    head_size = channels // HEADS
    blocks = to_windows(qkv_rows)
    split_heads = blocks.reshape(blocks.shape[:3] + (3, HEADS, head_size)).astype(jnp.float32)
    scores = jnp.einsum('abqhe,abkhe->abhqk', split_heads[:, :, :, 0], split_heads[:, :, :, 1]) * head_size ** (-0.5)
    labels = to_windows(window_tag[:, :, None])[..., 0]
    matched = labels[:, :, :, None] == labels[:, :, None, :]
    scores = jnp.where(matched[:, :, None], scores, -1e+30)
    weights = jax.nn.softmax(scores, axis=-1).astype(jnp.bfloat16)
    result = jnp.einsum('abhqk,abkhe->abqhe', weights.astype(jnp.float32), split_heads[:, :, :, 2])
    result = result.astype(jnp.bfloat16).reshape(blocks.shape[:3] + (channels,))
    return from_windows(result, height, breadth)

def window_block(stream, window_tag, w_qkv, w_out, w_up, w_down):
    qkv_rows = project(normalize(stream), w_qkv).astype(jnp.bfloat16)
    stream = stream + project(window_attention(qkv_rows, window_tag), w_out)
    hidden = jax.nn.gelu(project(normalize(stream), w_up), approximate=False).astype(jnp.bfloat16)
    return stream + project(hidden, w_down)

def member_block(stream, w_qkv, w_out):
    members, breadth, channels = stream.shape
    head_size = channels // HEADS
    qkv_rows = project(normalize(stream), w_qkv).astype(jnp.bfloat16)
    split_heads = qkv_rows.reshape(members, breadth, 3, HEADS, head_size).astype(jnp.float32)
    scores = jnp.einsum('mthe,nthe->thmn', split_heads[:, :, 0], split_heads[:, :, 1]) * head_size ** (-0.5)
    weights = jax.nn.softmax(scores, axis=-1).astype(jnp.bfloat16)
    result = jnp.einsum('thmn,nthe->mthe', weights.astype(jnp.float32), split_heads[:, :, 2])
    result = result.astype(jnp.bfloat16).reshape(members, breadth, channels)
    return stream + project(result, w_out)

def reference(fields, land_mask, offsets, land_embed, win_qkv, win_out, win_up, win_down, mem_qkv, mem_out, shift_qkv, shift_out, shift_up, shift_down):
    stream = fields.astype(jnp.float32) + land_mask.astype(jnp.float32)[None, :, :, None] * land_embed[None, None, None, :]
    no_groups = jnp.zeros((NLAT, NLON), jnp.int32)
    stream = lax.map(lambda member: window_block(member, no_groups, win_qkv, win_out, win_up, win_down), stream)
    stream = lax.map(lambda lat_row: member_block(lat_row, mem_qkv, mem_out), stream.transpose(1, 0, 2, 3)).transpose(1, 0, 2, 3)
    wrapped = ((jnp.arange(NLAT, dtype=jnp.int32) + offsets[0]) % NLAT < offsets[0]).astype(jnp.int32)
    window_tag = jnp.broadcast_to(wrapped[:, None], (NLAT, NLON))

    def shifted(member):
        rolled = jnp.roll(member, (-offsets[0], -offsets[1]), axis=(0, 1))
        finished = window_block(rolled, window_tag, shift_qkv, shift_out, shift_up, shift_down)
        return jnp.roll(finished, (offsets[0], offsets[1]), axis=(0, 1))
    stream = lax.map(shifted, stream)
    return stream.astype(jnp.bfloat16)
```

```python
import functools

import jax
import jax.numpy as jnp
from jax import lax
from jax.experimental import pallas as pl
from jax.experimental.pallas import tpu as pltpu
from jax.sharding import PartitionSpec as P

HEADS = 4
WIN = 8
LANES = 128
EPSILON = 1e-05
MASKED = -1e30
VMEM_LIMIT = 40 * 1024 * 1024

f32 = jnp.float32
bf16 = jnp.bfloat16


def normalize(stream):
    average = jnp.mean(stream, axis=-1, keepdims=True)
    centered = stream - average
    spread = jnp.mean(centered * centered, axis=-1, keepdims=True)
    return (centered * lax.rsqrt(spread + EPSILON)).astype(bf16)


def dot(a, b):
    return jnp.dot(a, b, preferred_element_type=f32)


def head_lanes(channels):
    return lax.broadcasted_iota(jnp.int32, (1, channels), 1) // (channels // HEADS)


def attend(query, key, value, bias):
    amount, channels = query.shape
    lanes = head_lanes(channels)
    scale = (channels // HEADS) ** (-0.5)
    stacked = jnp.concatenate(
        [query * jnp.where(lanes == head, scale, 0.0).astype(bf16) for head in range(HEADS)], axis=0
    )
    scores = lax.dot_general(stacked, key, (((1,), (1,)), ((), ())), preferred_element_type=f32)
    scores = scores.reshape(HEADS, amount, key.shape[0]) + bias[None]
    top = jnp.max(scores, axis=-1, keepdims=True)
    powers = jnp.exp(scores - top)
    total = jnp.sum(powers, axis=-1, keepdims=True)
    weights = (powers * (1.0 / total)).astype(bf16)
    mixed = dot(weights.reshape(HEADS * amount, key.shape[0]), value)
    result = mixed[:amount]
    for head in range(1, HEADS):
        result = jnp.where(lanes == head, mixed[head * amount : (head + 1) * amount], result)
    return result.astype(bf16)


def feed_forward(stream, up_ref, down_ref, chunk=256):
    normed = normalize(stream)
    total = stream
    for start in range(0, up_ref.shape[1], chunk):
        raw = dot(normed, up_ref[:, start : start + chunk])
        hidden = (0.5 * raw * (1.0 + lax.erf(raw * 0.5**0.5))).astype(bf16)
        total = total + dot(hidden, down_ref[start : start + chunk, :])
    return total


def window_kernel(
    shape, fields_ref, mask_ref, embed_ref, qkv_ref, out_ref, up_ref, down_ref,
    stream_ref, normed_ref, turned, held, attended,
):
    members, height, breadth, channels = shape
    rows = members * height
    for part in range(channels // LANES):
        turned[part] = fields_ref[:, part * LANES : (part + 1) * LANES].astype(f32)
    columns = []
    for column in range(breadth):
        taken = jnp.concatenate(
            [turned[part, pl.ds(column, rows, stride=breadth), :] for part in range(channels // LANES)],
            axis=1,
        ).reshape(members, height, channels)
        land = mask_ref[:, column : column + 1].astype(f32) * embed_ref[...]
        columns.append((taken + land[None]).reshape(rows, channels))
    stream = jnp.concatenate(columns, axis=0)
    held[...] = dot(normalize(stream), qkv_ref[...]).astype(bf16).reshape(breadth, rows, 3 * channels)
    tokens = breadth * height
    block = (lax.broadcasted_iota(jnp.int32, (tokens, tokens), 0) % height) // WIN
    other = (lax.broadcasted_iota(jnp.int32, (tokens, tokens), 1) % height) // WIN
    bias = jnp.where(block == other, 0.0, MASKED).astype(f32)
    for member in range(members):
        part = slice(member * height, (member + 1) * height)
        query, key, value = (
            held[:, part, i * channels : (i + 1) * channels].reshape(tokens, channels) for i in range(3)
        )
        attended[:, part, :] = attend(query, key, value, bias).reshape(breadth, height, channels)
    stream = stream + dot(attended[...].reshape(breadth * rows, channels), out_ref[...])
    stream = feed_forward(stream, up_ref, down_ref)
    stream_ref[...] = stream
    normed_ref[...] = normalize(stream)


def member_kernel(
    shape, stream_ref, *refs
):
    members, height, breadth, channels = shape
    *block_refs, qkv_ref, out_ref, late_ref, normed_ref, keys, queries, attended = refs
    rows = members * height
    amount = rows * len(block_refs)
    queries[...] = dot(block_refs[0][...], qkv_ref[:, :channels]).astype(bf16).reshape(
        breadth, rows, channels
    )
    for index, block_ref in enumerate(block_refs):
        keys[:, index * rows : (index + 1) * rows, :] = (
            dot(block_ref[...], qkv_ref[:, channels:]).astype(bf16).reshape(breadth, rows, 2 * channels)
        )
    row = lax.broadcasted_iota(jnp.int32, (rows, amount), 0) % height
    other = lax.broadcasted_iota(jnp.int32, (rows, amount), 1) % height
    bias = jnp.where(row == other, 0.0, MASKED).astype(f32)
    for column in range(breadth):
        attended[column] = attend(
            queries[column], keys[column, :, :channels], keys[column, :, channels:], bias
        )
    stream = stream_ref[...] + dot(attended[...].reshape(breadth * rows, channels), out_ref[...])
    late_ref[...] = stream
    normed_ref[...] = normalize(stream)


def shift_kernel(
    shape, place_ref, stream_ref, normed_ref, side_ref, edge_ref, corner_ref, qkv_ref, out_ref, up_ref,
    down_ref, updated_ref, held, beside, attended, turned,
):
    members, height, breadth, channels = shape
    rows, edge_rows = members * height, members * WIN
    tokens, edge_tokens = breadth * height, breadth * WIN
    held[...] = dot(normed_ref[...], qkv_ref[...]).astype(bf16).reshape(breadth, rows, 3 * channels)
    beside[...] = dot(side_ref[...], qkv_ref[:, channels:]).astype(bf16).reshape(
        breadth, rows, 2 * channels
    )
    edge = dot(edge_ref[...], qkv_ref[:, channels:]).reshape(breadth, edge_rows, 2 * channels)
    corner = dot(corner_ref[...], qkv_ref[:, channels:]).reshape(breadth, edge_rows, 2 * channels)

    lat_shift, lon_shift, first, last = place_ref[0], place_ref[1], place_ref[2], place_ref[3]
    amount = 2 * tokens + 2 * edge_tokens
    query_index = lax.broadcasted_iota(jnp.int32, (tokens, 1), 0)
    query_row, query_column = query_index % height, query_index // height
    query_tag = 2 * ((query_row - lat_shift + WIN) // WIN) + jnp.where(query_column >= lon_shift, 1, 0)
    index = lax.broadcasted_iota(jnp.int32, (1, amount), 1)
    whole = index < 2 * tokens
    local = jnp.where(whole, index % tokens, (index - 2 * tokens) % edge_tokens)
    mixed = jnp.where(whole, index // tokens, jnp.where(index < 2 * tokens + edge_tokens, 0, 1))
    key_row = jnp.where(whole, local % height, local % WIN)
    key_column = jnp.where(whole, local // height, local // WIN)
    edge_lat = jnp.where(
        key_row >= lat_shift, -1000 * first, height // WIN - 1000 * last
    )
    key_lat = jnp.where(whole, (key_row - lat_shift + WIN) // WIN, edge_lat)
    key_lon = jnp.where(key_column >= lon_shift, 1 - mixed, mixed)
    bias = jnp.where(query_tag == 2 * key_lat + key_lon, 0.0, MASKED).astype(f32)

    for member in range(members):
        part = slice(member * height, (member + 1) * height)
        edge_part = slice(member * WIN, (member + 1) * WIN)
        query = held[:, part, :channels].reshape(tokens, channels)
        pairs = []
        for i in range(2):
            lanes = slice(i * channels, (i + 1) * channels)
            lanes_held = slice((i + 1) * channels, (i + 2) * channels)
            pairs.append(
                jnp.concatenate(
                    [
                        held[:, part, lanes_held].reshape(tokens, channels),
                        beside[:, part, lanes].reshape(tokens, channels),
                        edge[:, edge_part, lanes].reshape(edge_tokens, channels).astype(bf16),
                        corner[:, edge_part, lanes].reshape(edge_tokens, channels).astype(bf16),
                    ],
                    axis=0,
                )
            )
        attended[:, part, :] = attend(query, pairs[0], pairs[1], bias).reshape(breadth, height, channels)
    stream = stream_ref[...] + dot(attended[...].reshape(breadth * rows, channels), out_ref[...])
    stream = feed_forward(stream, up_ref, down_ref)
    for column in range(breadth):
        for part in range(channels // LANES):
            turned[part, pl.ds(column, rows, stride=breadth), :] = stream[
                column * rows : (column + 1) * rows, part * LANES : (part + 1) * LANES
            ]
    for part in range(channels // LANES):
        updated_ref[:, part * LANES : (part + 1) * LANES] = turned[part].astype(bf16)


def in_vmem(count):
    return [pl.BlockSpec(memory_space=pltpu.VMEM)] * count


def per_device(
    fields, land_mask, offsets, land_embed, win_qkv, win_out, win_up, win_down, mem_qkv, mem_out,
    shift_qkv, shift_out, shift_up, shift_down,
):
    shape = fields.shape
    members, height, breadth, channels = shape
    rows, tokens = members * height, members * height * breadth
    params = pltpu.CompilerParams(vmem_limit_bytes=VMEM_LIMIT)
    stream, normed = pl.pallas_call(
        functools.partial(window_kernel, shape),
        out_shape=(
            jax.ShapeDtypeStruct((tokens, channels), f32),
            jax.ShapeDtypeStruct((tokens, channels), bf16),
        ),
        in_specs=in_vmem(7),
        out_specs=tuple(in_vmem(2)),
        scratch_shapes=[
            pltpu.VMEM((channels // LANES, tokens, LANES), f32),
            pltpu.VMEM((breadth, rows, 3 * channels), bf16),
            pltpu.VMEM((breadth, rows, channels), bf16),
        ],
        compiler_params=params,
    )(
        fields.reshape(tokens, channels), land_mask, land_embed.reshape(1, channels),
        win_qkv, win_out, win_up, win_down,
    )

    groups = lax.axis_size("member")
    blocks = [normed]
    bit = 1
    while bit < groups:
        bit *= 2
    while bit > 1:
        bit //= 2
        partner = [(i, i ^ bit) for i in range(groups)]
        blocks = blocks + [lax.ppermute(block, "member", partner) for block in blocks]

    late, normed = pl.pallas_call(
        functools.partial(member_kernel, shape),
        out_shape=(
            jax.ShapeDtypeStruct((tokens, channels), f32),
            jax.ShapeDtypeStruct((tokens, channels), bf16),
        ),
        in_specs=in_vmem(3 + len(blocks)),
        out_specs=tuple(in_vmem(2)),
        scratch_shapes=[
            pltpu.VMEM((breadth, rows * groups, 2 * channels), bf16),
            pltpu.VMEM((breadth, rows, channels), bf16),
            pltpu.VMEM((breadth, rows, channels), bf16),
        ],
        compiler_params=params,
    )(stream, *blocks, mem_qkv, mem_out)

    lat_count, lon_count = lax.axis_size("lat"), lax.axis_size("lon")
    lat_index = lax.axis_index("lat")
    ring = [(i, (i + 1) % lon_count) for i in range(lon_count)]
    back = [(b, a) for a, b in ring]
    own = normed.reshape(breadth, members, height, channels)
    top, bottom = own[:, :, :WIN], own[:, :, height - WIN :]
    down = [(i, i + 1) for i in range(lat_count - 1)]
    up = [(b, a) for a, b in down]
    if lat_count == 2:
        sends = [(jnp.where(lat_index == 0, bottom, top), down + up)]
    else:
        sends = [(bottom, down), (top, up)]

    def both_ways(amount, own, *edges):
        def along(block, lat_pairs):
            if lat_pairs is None:
                low = lax.ppermute(block[amount:], "lon", ring)
                high = lax.ppermute(block[:amount], "lon", back)
            else:
                low, high = (
                    lax.ppermute(
                        piece,
                        ("lat", "lon"),
                        [
                            (a * lon_count + c, b * lon_count + d)
                            for a, b in lat_pairs
                            for c, d in lon_pairs
                        ],
                    )
                    for piece, lon_pairs in ((block[amount:], ring), (block[:amount], back))
                )
            return jnp.concatenate([high, low], axis=0)

        straight = [lax.ppermute(block, "lat", pairs) for block, (_, pairs) in zip(edges, sends)]
        corners = [along(block, pairs) for block, (_, pairs) in zip(edges, sends)]
        return [along(own, None)] + straight + corners

    received = lax.switch(
        offsets[1] - 1,
        [functools.partial(both_ways, amount) for amount in range(1, WIN)],
        own, *[block for block, _ in sends],
    )
    side = received[0]
    count = len(sends)
    if count == 1:
        edge, corner = received[1], received[2]
    else:
        chosen = (jnp.arange(WIN, dtype=jnp.int32) >= offsets[0])[None, None, :, None]
        edge = jnp.where(chosen, received[1], received[2])
        corner = jnp.where(chosen, received[3], received[4])

    place = jnp.concatenate(
        [
            offsets,
            jnp.stack([lat_index == 0, lat_index == lat_count - 1]).astype(jnp.int32),
        ]
    )
    updated = pl.pallas_call(
        functools.partial(shift_kernel, shape),
        out_shape=jax.ShapeDtypeStruct((tokens, channels), bf16),
        in_specs=[pl.BlockSpec(memory_space=pltpu.SMEM)] + in_vmem(9),
        out_specs=pl.BlockSpec(memory_space=pltpu.VMEM),
        scratch_shapes=[
            pltpu.VMEM((breadth, rows, 3 * channels), bf16),
            pltpu.VMEM((breadth, rows, 2 * channels), bf16),
            pltpu.VMEM((breadth, rows, channels), bf16),
            pltpu.VMEM((channels // LANES, tokens, LANES), f32),
        ],
        compiler_params=params,
    )(
        place, late, normed, side.reshape(tokens, channels), edge.reshape(-1, channels),
        corner.reshape(-1, channels), shift_qkv, shift_out, shift_up, shift_down,
    )
    return updated.reshape(shape)


def solution(mesh):
    return jax.shard_map(
        per_device,
        mesh=mesh,
        in_specs=(P("member", "lat", "lon", None), P("lat", "lon")) + (P(),) * 12,
        out_specs=P("member", "lat", "lon", None),
        check_vma=False,
    )
```

```python
import functools

import jax
import jax.numpy as jnp
from jax import lax
from jax.experimental import pallas as pl
from jax.experimental.pallas import tpu as pltpu
from jax.sharding import PartitionSpec as P

HEADS = 4
WIN = 8
LANES = 128
EPSILON = 1e-05
MASKED = -1e30
VMEM_LIMIT = 40 * 1024 * 1024

f32 = jnp.float32
bf16 = jnp.bfloat16


def normalize(stream):
    average = jnp.mean(stream, axis=-1, keepdims=True)
    centered = stream - average
    spread = jnp.mean(centered * centered, axis=-1, keepdims=True)
    return (centered * lax.rsqrt(spread + EPSILON)).astype(bf16)


def dot(a, b):
    return jnp.dot(a, b, preferred_element_type=f32)


def head_lanes(channels):
    return lax.broadcasted_iota(jnp.int32, (1, channels), 1) // (channels // HEADS)


def attend(query, key, value, bias):
    amount, channels = query.shape
    lanes = head_lanes(channels)
    scale = (channels // HEADS) ** (-0.5)
    stacked = jnp.concatenate(
        [query * jnp.where(lanes == head, scale, 0.0).astype(bf16) for head in range(HEADS)], axis=0
    )
    scores = lax.dot_general(stacked, key, (((1,), (1,)), ((), ())), preferred_element_type=f32)
    scores = scores.reshape(HEADS, amount, key.shape[0]) + bias[None]
    top = jnp.max(scores, axis=-1, keepdims=True)
    powers = jnp.exp(scores - top)
    total = jnp.sum(powers, axis=-1, keepdims=True)
    weights = (powers * (1.0 / total)).astype(bf16)
    mixed = dot(weights.reshape(HEADS * amount, key.shape[0]), value)
    result = mixed[:amount]
    for head in range(1, HEADS):
        result = jnp.where(lanes == head, mixed[head * amount : (head + 1) * amount], result)
    return result.astype(bf16)


def feed_forward(stream, up_ref, down_ref, chunk=256):
    normed = normalize(stream)
    total = stream
    for start in range(0, up_ref.shape[1], chunk):
        raw = dot(normed, up_ref[:, start : start + chunk])
        hidden = (0.5 * raw * (1.0 + lax.erf(raw * 0.5**0.5))).astype(bf16)
        total = total + dot(hidden, down_ref[start : start + chunk, :])
    return total


def window_kernel(
    shape, *refs
):
    members, height, breadth, channels = shape
    sources, refs = refs[:7], refs[7:]
    stream_ref, normed_ref, *places, semaphores, turned, held, attended = refs
    copies = [
        pltpu.make_async_copy(source, place, semaphores.at[index])
        for index, (source, place) in enumerate(zip(sources, places))
    ]
    for copy in copies:
        copy.start()
    fields_ref, land_ref, embed_ref, qkv_ref, out_ref, up_ref, down_ref = places
    rows = members * height
    for copy in copies[:3]:
        copy.wait()
    for part in range(channels // LANES):
        turned[part] = fields_ref[:, part * LANES : (part + 1) * LANES].astype(f32)
    same = lax.broadcasted_iota(jnp.int32, (1, height, height), 1) == lax.broadcasted_iota(
        jnp.int32, (1, height, height), 2
    )
    land = jnp.sum(
        jnp.where(same, land_ref[...].astype(f32)[:, None, :], 0.0), axis=-1, keepdims=True
    )
    columns = []
    for column in range(breadth):
        taken = jnp.concatenate(
            [turned[part, pl.ds(column, rows, stride=breadth), :] for part in range(channels // LANES)],
            axis=1,
        ).reshape(members, height, channels)
        columns.append((taken + (land[column] * embed_ref[...])[None]).reshape(rows, channels))
    stream = jnp.concatenate(columns, axis=0)
    normed = normalize(stream)
    copies[3].wait()
    held[...] = dot(normed, qkv_ref[...]).astype(bf16).reshape(breadth, rows, 3 * channels)
    tokens = breadth * height
    block = (lax.broadcasted_iota(jnp.int32, (tokens, tokens), 0) % height) // WIN
    other = (lax.broadcasted_iota(jnp.int32, (tokens, tokens), 1) % height) // WIN
    bias = jnp.where(block == other, 0.0, MASKED).astype(f32)
    for member in range(members):
        part = slice(member * height, (member + 1) * height)
        query, key, value = (
            held[:, part, i * channels : (i + 1) * channels].reshape(tokens, channels) for i in range(3)
        )
        attended[:, part, :] = attend(query, key, value, bias).reshape(breadth, height, channels)
    for copy in copies[4:]:
        copy.wait()
    stream = stream + dot(attended[...].reshape(breadth * rows, channels), out_ref[...])
    stream = feed_forward(stream, up_ref, down_ref)
    stream_ref[...] = stream
    normed_ref[...] = normalize(stream)


def near_kernel(shape, *refs):
    members, height, breadth, channels = shape
    *block_refs, qkv_ref, queries_ref, pairs_ref = refs
    rows = members * height
    queries_ref[...] = (
        dot(block_refs[0][...], qkv_ref[:, :channels]).astype(bf16).reshape(breadth, rows, channels)
    )
    for index, block_ref in enumerate(block_refs):
        pairs_ref[:, index * rows : (index + 1) * rows, :] = (
            dot(block_ref[...], qkv_ref[:, channels:]).astype(bf16).reshape(breadth, rows, 2 * channels)
        )


def member_kernel(shape, lat_count, stream_ref, queries_ref, pairs_ref, *refs):
    members, height, breadth, channels = shape
    sides = 1 if lat_count == 2 else 2
    *block_refs, qkv_ref, out_ref = refs[: -4 - sides]
    late_ref, normed_ref, *edge_refs = refs[-4 - sides : -2]
    far, attended = refs[-2:]
    rows = members * height
    amount = rows * len(block_refs) + pairs_ref.shape[1]
    for index, block_ref in enumerate(block_refs):
        far[:, index * rows : (index + 1) * rows, :] = (
            dot(block_ref[...], qkv_ref[:, channels:]).astype(bf16).reshape(breadth, rows, 2 * channels)
        )
    row = lax.broadcasted_iota(jnp.int32, (rows, amount), 0) % height
    other = lax.broadcasted_iota(jnp.int32, (rows, amount), 1) % height
    bias = jnp.where(row == other, 0.0, MASKED).astype(f32)
    for column in range(breadth):
        both = jnp.concatenate([pairs_ref[column], far[column]], axis=0)
        attended[column] = attend(queries_ref[column], both[:, :channels], both[:, channels:], bias)
    stream = stream_ref[...] + dot(attended[...].reshape(breadth * rows, channels), out_ref[...])
    late_ref[...] = stream
    normed = normalize(stream)
    normed_ref[...] = normed
    lines = normed.astype(f32).reshape(breadth * members, height, channels)
    for edge_ref, edge in zip(edge_refs, lat_ends(lines, lat_count)):
        edge_ref[...] = edge.reshape(breadth * members * WIN, channels).astype(bf16)


def per_member(lines, members, breadth):
    lines = lines.reshape(breadth, members * WIN, lines.shape[-1])
    return [
        lines[:, member * WIN : (member + 1) * WIN].reshape(breadth * WIN, lines.shape[-1]).astype(bf16)
        for member in range(members)
    ]


def join_kernel(shape, lat_count, amount, first_ref, second_ref, side_ref, *end_refs):
    members, height, breadth, channels = shape
    high_ref, low_ref = (first_ref, second_ref) if 2 * amount <= breadth else (second_ref, first_ref)
    side_ref[:amount] = high_ref[...]
    side_ref[amount:] = low_ref[...]
    for part, block_ref in ((slice(0, amount), high_ref), (slice(amount, breadth), low_ref)):
        columns = part.stop - part.start
        lines = block_ref[...].astype(f32).reshape(columns * members, height, channels)
        for end_ref, end in zip(end_refs, lat_ends(lines, lat_count)):
            place = slice(part.start * members * WIN, part.stop * members * WIN)
            end_ref[place, :] = end.reshape(columns * members * WIN, channels).astype(bf16)


def lat_ends(lines, lat_count):
    top, bottom = lines[:, :WIN], lines[:, lines.shape[1] - WIN :]
    if lat_count == 2:
        return [jnp.where(lax.axis_index("lat") == 0, bottom, top)]
    return [bottom, top]


def early_kernel(shape, normed_ref, side_ref, edge_ref, qkv_ref, held_ref, beside_ref, across_ref):
    members, height, breadth, channels = shape
    rows = members * height
    held_ref[...] = dot(normed_ref[...], qkv_ref[...]).astype(bf16).reshape(breadth, rows, 3 * channels)
    beside_ref[...] = dot(side_ref[...], qkv_ref[:, channels:]).astype(bf16).reshape(
        breadth, rows, 2 * channels
    )
    edge = per_member(dot(edge_ref[...], qkv_ref[:, channels:]), members, breadth)
    for member in range(members):
        across_ref[member] = edge[member]


def corner_kernel(shape, corner_ref, qkv_ref, corner_pairs_ref):
    members, height, breadth, channels = shape
    corner = per_member(dot(corner_ref[...], qkv_ref[:, channels:]), members, breadth)
    for member in range(members):
        corner_pairs_ref[member] = corner[member]


def shift_kernel(
    shape, lat_count, place_ref, stream_ref, held, beside, across, corner, out_ref, up_ref, down_ref,
    updated_ref, attended, turned,
):
    members, height, breadth, channels = shape
    rows = members * height
    tokens, edge_tokens = breadth * height, breadth * WIN

    lat_shift, lon_shift = place_ref[0], place_ref[1]
    first = jnp.where(lax.axis_index("lat") == 0, 1, 0)
    last = jnp.where(lax.axis_index("lat") == lat_count - 1, 1, 0)
    amount = 2 * tokens + 2 * edge_tokens
    query_index = lax.broadcasted_iota(jnp.int32, (tokens, 1), 0)
    query_row, query_column = query_index % height, query_index // height
    query_tag = 2 * ((query_row - lat_shift + WIN) // WIN) + jnp.where(query_column >= lon_shift, 1, 0)
    index = lax.broadcasted_iota(jnp.int32, (1, amount), 1)
    whole = index < 2 * tokens
    local = jnp.where(whole, index % tokens, (index - 2 * tokens) % edge_tokens)
    mixed = jnp.where(whole, index // tokens, jnp.where(index < 2 * tokens + edge_tokens, 0, 1))
    key_row = jnp.where(whole, local % height, local % WIN)
    key_column = jnp.where(whole, local // height, local // WIN)
    edge_lat = jnp.where(key_row >= lat_shift, -1000 * first, height // WIN - 1000 * last)
    key_lat = jnp.where(whole, (key_row - lat_shift + WIN) // WIN, edge_lat)
    key_lon = jnp.where(key_column >= lon_shift, 1 - mixed, mixed)
    bias = jnp.where(query_tag == 2 * key_lat + key_lon, 0.0, MASKED).astype(f32)

    for member in range(members):
        part = slice(member * height, (member + 1) * height)
        query = held[:, part, :channels].reshape(tokens, channels)
        pairs = []
        for i in range(2):
            lanes = slice(i * channels, (i + 1) * channels)
            pairs.append(
                jnp.concatenate(
                    [
                        held[:, part, (i + 1) * channels : (i + 2) * channels].reshape(tokens, channels),
                        beside[:, part, lanes].reshape(tokens, channels),
                        across[member, :, lanes],
                        corner[member, :, lanes],
                    ],
                    axis=0,
                )
            )
        attended[:, part, :] = attend(query, pairs[0], pairs[1], bias).reshape(breadth, height, channels)
    stream = stream_ref[...] + dot(attended[...].reshape(breadth * rows, channels), out_ref[...])
    stream = feed_forward(stream, up_ref, down_ref)
    for column in range(breadth):
        for part in range(channels // LANES):
            turned[part, pl.ds(column, rows, stride=breadth), :] = stream[
                column * rows : (column + 1) * rows, part * LANES : (part + 1) * LANES
            ]
    for part in range(channels // LANES):
        updated_ref[:, part * LANES : (part + 1) * LANES] = turned[part].astype(bf16)


def in_vmem(count):
    return [pl.BlockSpec(memory_space=pltpu.VMEM)] * count


def per_device(
    fields, land_mask, offsets, land_embed, win_qkv, win_out, win_up, win_down, mem_qkv, mem_out,
    shift_qkv, shift_out, shift_up, shift_down,
):
    shape = fields.shape
    members, height, breadth, channels = shape
    rows, tokens = members * height, members * height * breadth
    edge_tokens = members * WIN * breadth
    params = pltpu.CompilerParams(vmem_limit_bytes=VMEM_LIMIT)
    sources = (
        fields.reshape(tokens, channels), land_mask.T, land_embed.reshape(1, channels),
        win_qkv, win_out, win_up, win_down,
    )
    stream, normed = pl.pallas_call(
        functools.partial(window_kernel, shape),
        out_shape=(
            jax.ShapeDtypeStruct((tokens, channels), f32),
            jax.ShapeDtypeStruct((tokens, channels), bf16),
        ),
        in_specs=[pl.BlockSpec(memory_space=pltpu.HBM)] * len(sources),
        out_specs=tuple(in_vmem(2)),
        scratch_shapes=[pltpu.VMEM(source.shape, source.dtype) for source in sources]
        + [
            pltpu.SemaphoreType.DMA((len(sources),)),
            pltpu.VMEM((channels // LANES, tokens, LANES), f32),
            pltpu.VMEM((breadth, rows, 3 * channels), bf16),
            pltpu.VMEM((breadth, rows, channels), bf16),
        ],
        compiler_params=pltpu.CompilerParams(vmem_limit_bytes=60 * 1024 * 1024),
    )(*sources)

    groups = lax.axis_size("member")
    blocks = [normed]
    bit = 1
    while bit * 2 < groups:
        bit *= 2
    far = [lax.ppermute(normed, "member", [(i, i ^ bit) for i in range(groups)])]
    near = []
    partners = []
    while bit > 1:
        bit //= 2
        partners.append([(i, i ^ bit) for i in range(groups)])
        near = near + [lax.ppermute(block, "member", partners[-1]) for block in blocks + near]

    queries, pairs = pl.pallas_call(
        functools.partial(near_kernel, shape),
        out_shape=(
            jax.ShapeDtypeStruct((breadth, rows, channels), bf16),
            jax.ShapeDtypeStruct((breadth, rows * len(blocks), 2 * channels), bf16),
        ),
        in_specs=in_vmem(1 + len(blocks)),
        out_specs=tuple(in_vmem(2)),
        compiler_params=params,
        cost_estimate=pl.CostEstimate(
            flops=2 * tokens * channels * channels * (1 + 2 * len(blocks)),
            bytes_accessed=2 * tokens * channels * 6,
            transcendentals=0,
        ),
    )(*blocks, mem_qkv)
    branch = offsets[1] - 1
    far[0], branch, queries, pairs = lax.optimization_barrier((far[0], branch, queries, pairs))
    for partner in partners:
        far = far + [lax.ppermute(block, "member", partner) for block in far]
    far = near + far

    lat_count, lon_count = lax.axis_size("lat"), lax.axis_size("lon")
    lat_index = lax.axis_index("lat")
    down = [(i, i + 1) for i in range(lat_count - 1)]
    up = [(b, a) for a, b in down]
    lat_pairs = [down + up] if lat_count == 2 else [down, up]
    late, normed, *edges = pl.pallas_call(
        functools.partial(member_kernel, shape, lat_count),
        out_shape=(
            jax.ShapeDtypeStruct((tokens, channels), f32),
            jax.ShapeDtypeStruct((tokens, channels), bf16),
        )
        + (jax.ShapeDtypeStruct((edge_tokens, channels), bf16),) * len(lat_pairs),
        in_specs=in_vmem(5 + len(far)),
        out_specs=tuple(in_vmem(2 + len(lat_pairs))),
        scratch_shapes=[
            pltpu.VMEM((breadth, rows * len(far), 2 * channels), bf16),
            pltpu.VMEM((breadth, rows, channels), bf16),
        ],
        compiler_params=params,
    )(stream, queries, pairs, *far, mem_qkv, mem_out)

    ring = [(i, (i + 1) % lon_count) for i in range(lon_count)]
    back = [(b, a) for a, b in ring]

    def gather(amount, own, *edges):
        low = lax.ppermute(own[amount:], "lon", ring)
        high = lax.ppermute(own[:amount], "lon", back)
        straight = [lax.ppermute(edge, "lat", pairs) for edge, pairs in zip(edges, lat_pairs)]
        end_shape = jax.ShapeDtypeStruct((edge_tokens, channels), bf16)
        side, *ends = pl.pallas_call(
            functools.partial(join_kernel, shape, lat_count, amount),
            out_shape=(jax.ShapeDtypeStruct((breadth, rows, channels), bf16),)
            + (end_shape,) * len(lat_pairs),
            in_specs=in_vmem(2),
            out_specs=tuple(in_vmem(1 + len(lat_pairs))),
            compiler_params=params,
        )(*((high, low) if 2 * amount <= breadth else (low, high)))
        corners = [lax.ppermute(end, "lat", pairs) for end, pairs in zip(ends, lat_pairs)]
        if lat_count == 2:
            edge, corner = straight[0], corners[0]
        else:
            above = jnp.tile(jnp.arange(WIN, dtype=jnp.int32) >= offsets[0], breadth * members)[:, None]
            edge, corner = jnp.where(above, *straight), jnp.where(above, *corners)

        pairs_shape = jax.ShapeDtypeStruct((members, breadth * WIN, 2 * channels), bf16)
        corner = pl.pallas_call(
            functools.partial(corner_kernel, shape),
            out_shape=pairs_shape,
            in_specs=in_vmem(2),
            out_specs=in_vmem(1)[0],
            compiler_params=params,
        )(corner, shift_qkv)
        return pl.pallas_call(
            functools.partial(early_kernel, shape),
            out_shape=(
                jax.ShapeDtypeStruct((breadth, rows, 3 * channels), bf16),
                jax.ShapeDtypeStruct((breadth, rows, 2 * channels), bf16),
                pairs_shape,
            ),
            in_specs=in_vmem(4),
            out_specs=tuple(in_vmem(3)),
            compiler_params=params,
            cost_estimate=pl.CostEstimate(
                flops=2 * tokens * channels * channels * 6,
                bytes_accessed=2 * tokens * channels * 8,
                transcendentals=0,
            ),
        )(own.reshape(tokens, channels), side.reshape(tokens, channels), edge, shift_qkv) + (corner,)

    held, beside, across, corner = lax.switch(
        branch,
        [functools.partial(gather, amount) for amount in range(1, WIN)],
        normed.reshape(breadth, rows, channels), *edges,
    )
    updated = pl.pallas_call(
        functools.partial(shift_kernel, shape, lat_count),
        out_shape=jax.ShapeDtypeStruct((tokens, channels), bf16),
        in_specs=[pl.BlockSpec(memory_space=pltpu.SMEM)] + in_vmem(8),
        out_specs=pl.BlockSpec(memory_space=pltpu.VMEM),
        scratch_shapes=[
            pltpu.VMEM((breadth, rows, channels), bf16),
            pltpu.VMEM((channels // LANES, tokens, LANES), f32),
        ],
        compiler_params=params,
    )(
        offsets, late, held, beside, across, corner, shift_out, shift_up, shift_down,
    )
    return updated.reshape(shape)


def solution(mesh):
    return jax.shard_map(
        per_device,
        mesh=mesh,
        in_specs=(P("member", "lat", "lon", None), P("lat", "lon")) + (P(),) * 12,
        out_specs=P("member", "lat", "lon", None),
        check_vma=False,
    )
```

```python
import functools

import jax
import jax.numpy as jnp
from jax import lax
from jax.experimental import pallas as pl
from jax.experimental.pallas import tpu as pltpu
from jax.sharding import PartitionSpec as P

HEADS = 4
WIN = 8
LANES = 128
EPSILON = 1e-05
MASKED = -1e30
VMEM_LIMIT = 40 * 1024 * 1024

f32 = jnp.float32
bf16 = jnp.bfloat16


def normalize(stream):
    average = jnp.mean(stream, axis=-1, keepdims=True)
    centered = stream - average
    spread = jnp.mean(centered * centered, axis=-1, keepdims=True)
    return (centered * lax.rsqrt(spread + EPSILON)).astype(bf16)


def dot(a, b):
    return jnp.dot(a, b, preferred_element_type=f32)


def head_lanes(channels):
    return lax.broadcasted_iota(jnp.int32, (1, channels), 1) // (channels // HEADS)


def partial_attention(query, key, value, bias):
    amount, channels = query.shape
    lanes = head_lanes(channels)
    scale = (channels // HEADS) ** (-0.5)
    stacked = jnp.concatenate(
        [query * jnp.where(lanes == head, scale, 0.0).astype(bf16) for head in range(HEADS)], axis=0
    )
    scores = lax.dot_general(stacked, key, (((1,), (1,)), ((), ())), preferred_element_type=f32)
    scores = scores.reshape(HEADS, amount, key.shape[0]) + bias[None]
    top = jnp.max(scores, axis=-1, keepdims=True)
    powers = jnp.exp(scores - top)
    total = jnp.sum(powers, axis=-1, keepdims=True)
    mixed = dot(powers.astype(bf16).reshape(HEADS * amount, key.shape[0]), value)

    def in_lanes(parts):
        result = parts[0]
        for head in range(1, HEADS):
            result = jnp.where(lanes == head, parts[head], result)
        return jnp.broadcast_to(result, (amount, channels))

    return in_lanes(mixed.reshape(HEADS, amount, channels)), in_lanes(top), in_lanes(total)


def joined_attention(one, two):
    top = jnp.maximum(one[1], two[1])
    first, second = jnp.exp(one[1] - top), jnp.exp(two[1] - top)
    return (first * one[0] + second * two[0]) / (first * one[2] + second * two[2])


def attend(query, key, value, bias):
    mixed, _, total = partial_attention(query, key, value, bias)
    return (mixed / total).astype(bf16)


def feed_forward(stream, up_ref, down_ref, chunk=256):
    normed = normalize(stream)
    total = stream
    for start in range(0, up_ref.shape[1], chunk):
        raw = dot(normed, up_ref[:, start : start + chunk])
        hidden = (0.5 * raw * (1.0 + lax.erf(raw * 0.5**0.5))).astype(bf16)
        total = total + dot(hidden, down_ref[start : start + chunk, :])
    return total


def window_kernel(
    shape, *refs
):
    members, height, breadth, channels = shape
    sources, refs = refs[:7], refs[7:]
    stream_ref, normed_ref, *places, semaphores, turned, held, attended = refs
    copies = [
        pltpu.make_async_copy(source, place, semaphores.at[index])
        for index, (source, place) in enumerate(zip(sources, places))
    ]
    for copy in copies:
        copy.start()
    fields_ref, land_ref, embed_ref, qkv_ref, out_ref, up_ref, down_ref = places
    rows = members * height
    for copy in copies[:3]:
        copy.wait()
    for part in range(channels // LANES):
        turned[part] = fields_ref[:, part * LANES : (part + 1) * LANES].astype(f32)
    same = lax.broadcasted_iota(jnp.int32, (1, height, height), 1) == lax.broadcasted_iota(
        jnp.int32, (1, height, height), 2
    )
    land = jnp.sum(
        jnp.where(same, land_ref[...].astype(f32)[:, None, :], 0.0), axis=-1, keepdims=True
    )
    columns = []
    for column in range(breadth):
        taken = jnp.concatenate(
            [turned[part, pl.ds(column, rows, stride=breadth), :] for part in range(channels // LANES)],
            axis=1,
        ).reshape(members, height, channels)
        columns.append((taken + (land[column] * embed_ref[...])[None]).reshape(rows, channels))
    stream = jnp.concatenate(columns, axis=0)
    normed = normalize(stream)
    copies[3].wait()
    held[...] = dot(normed, qkv_ref[...]).astype(bf16).reshape(breadth, rows, 3 * channels)
    tokens = breadth * height
    block = (lax.broadcasted_iota(jnp.int32, (tokens, tokens), 0) % height) // WIN
    other = (lax.broadcasted_iota(jnp.int32, (tokens, tokens), 1) % height) // WIN
    bias = jnp.where(block == other, 0.0, MASKED).astype(f32)
    for member in range(members):
        part = slice(member * height, (member + 1) * height)
        query, key, value = (
            held[:, part, i * channels : (i + 1) * channels].reshape(tokens, channels) for i in range(3)
        )
        attended[:, part, :] = attend(query, key, value, bias).reshape(breadth, height, channels)
    for copy in copies[4:]:
        copy.wait()
    stream = stream + dot(attended[...].reshape(breadth * rows, channels), out_ref[...])
    stream = feed_forward(stream, up_ref, down_ref)
    stream_ref[...] = stream
    normed_ref[...] = normalize(stream)


def member_pairs(shape, block_refs, qkv_ref, pairs):
    members, height, breadth, channels = shape
    rows = members * height
    for index, block_ref in enumerate(block_refs):
        pairs[:, index * rows : (index + 1) * rows, :] = (
            dot(block_ref[...], qkv_ref[:, channels:]).astype(bf16).reshape(breadth, rows, 2 * channels)
        )
    amount = pairs.shape[1]
    row = lax.broadcasted_iota(jnp.int32, (rows, amount), 0) % height
    other = lax.broadcasted_iota(jnp.int32, (rows, amount), 1) % height
    return jnp.where(row == other, 0.0, MASKED).astype(f32)


def near_kernel(shape, *refs):
    members, height, breadth, channels = shape
    *block_refs, qkv_ref, queries_ref, mixed_ref, top_ref, total_ref, pairs = refs
    rows = members * height
    queries_ref[...] = (
        dot(block_refs[0][...], qkv_ref[:, :channels]).astype(bf16).reshape(breadth, rows, channels)
    )
    bias = member_pairs(shape, block_refs, qkv_ref, pairs)
    for column in range(breadth):
        mixed_ref[column], top_ref[column], total_ref[column] = partial_attention(
            queries_ref[column], pairs[column, :, :channels], pairs[column, :, channels:], bias
        )


def member_kernel(shape, lat_count, stream_ref, queries_ref, mixed_ref, top_ref, total_ref, *refs):
    members, height, breadth, channels = shape
    sides = 1 if lat_count == 2 else 2
    *block_refs, qkv_ref, out_ref = refs[: -4 - sides]
    late_ref, normed_ref, *edge_refs = refs[-4 - sides : -2]
    pairs, attended = refs[-2:]
    rows = members * height
    bias = member_pairs(shape, block_refs, qkv_ref, pairs)
    for column in range(breadth):
        far = partial_attention(
            queries_ref[column], pairs[column, :, :channels], pairs[column, :, channels:], bias
        )
        near = mixed_ref[column], top_ref[column], total_ref[column]
        attended[column] = joined_attention(near, far).astype(bf16)
    stream = stream_ref[...] + dot(attended[...].reshape(breadth * rows, channels), out_ref[...])
    late_ref[...] = stream
    normed = normalize(stream)
    normed_ref[...] = normed
    lines = normed.astype(f32).reshape(breadth * members, height, channels)
    for edge_ref, edge in zip(edge_refs, lat_ends(lines, lat_count)):
        edge_ref[...] = edge.reshape(breadth * members * WIN, channels).astype(bf16)


def per_member(lines, members, breadth):
    lines = lines.reshape(breadth, members * WIN, lines.shape[-1])
    return [
        lines[:, member * WIN : (member + 1) * WIN].reshape(breadth * WIN, lines.shape[-1]).astype(bf16)
        for member in range(members)
    ]


def join_kernel(shape, lat_count, amount, first_ref, second_ref, side_ref, *end_refs):
    members, height, breadth, channels = shape
    high_ref, low_ref = (first_ref, second_ref) if 2 * amount <= breadth else (second_ref, first_ref)
    side_ref[:amount] = high_ref[...]
    side_ref[amount:] = low_ref[...]
    for part, block_ref in ((slice(0, amount), high_ref), (slice(amount, breadth), low_ref)):
        columns = part.stop - part.start
        lines = block_ref[...].astype(f32).reshape(columns * members, height, channels)
        for end_ref, end in zip(end_refs, lat_ends(lines, lat_count)):
            place = slice(part.start * members * WIN, part.stop * members * WIN)
            end_ref[place, :] = end.reshape(columns * members * WIN, channels).astype(bf16)


def lat_ends(lines, lat_count):
    top, bottom = lines[:, :WIN], lines[:, lines.shape[1] - WIN :]
    if lat_count == 2:
        return [jnp.where(lax.axis_index("lat") == 0, bottom, top)]
    return [bottom, top]


def lat_window(row, place_ref):
    return (row - place_ref[:, :1] + WIN) // WIN


def shifted_bias(shape, place_ref, key_lat, key_lon):
    members, height, breadth, channels = shape
    index = lax.broadcasted_iota(jnp.int32, (breadth * height, 1), 0)
    query_lon = jnp.where(index // height >= place_ref[:, 1:], 1, 0)
    query_tag = 2 * lat_window(index % height, place_ref) + query_lon
    return jnp.where(query_tag == 2 * key_lat + key_lon, 0.0, MASKED).astype(f32)


def early_kernel(
    shape, lat_count, place_ref, normed_ref, side_ref, edge_ref, qkv_ref,
    queries_ref, mixed_ref, top_ref, total_ref, across_ref, late_bias_ref, held, beside,
):
    members, height, breadth, channels = shape
    rows, tokens = members * height, breadth * height
    held[...] = dot(normed_ref[...], qkv_ref[...]).astype(bf16).reshape(breadth, rows, 3 * channels)
    beside[...] = dot(side_ref[...], qkv_ref[:, channels:]).astype(bf16).reshape(
        breadth, rows, 2 * channels
    )
    edge = per_member(dot(edge_ref[...], qkv_ref[:, channels:]), members, breadth)
    index = lax.broadcasted_iota(jnp.int32, (1, 2 * tokens), 1)
    mixed, local = index // tokens, index % tokens
    key_lon = jnp.where(local // height >= place_ref[:, 1:], 1 - mixed, mixed)
    bias = shifted_bias(shape, place_ref, lat_window(local % height, place_ref), key_lon)
    for member in range(members):
        across_ref[member] = edge[member]
        part = slice(member * height, (member + 1) * height)
        query = held[:, part, :channels].reshape(tokens, channels)
        queries_ref[member] = query
        key, value = (
            jnp.concatenate(
                [
                    held[:, part, (i + 1) * channels : (i + 2) * channels].reshape(tokens, channels),
                    beside[:, part, i * channels : (i + 1) * channels].reshape(tokens, channels),
                ],
                axis=0,
            )
            for i in range(2)
        )
        mixed_ref[member], top_ref[member], total_ref[member] = partial_attention(query, key, value, bias)

    edge_tokens = breadth * WIN
    first = jnp.where(lax.axis_index("lat") == 0, 1, 0)
    last = jnp.where(lax.axis_index("lat") == lat_count - 1, 1, 0)
    index = lax.broadcasted_iota(jnp.int32, (1, 2 * edge_tokens), 1)
    mixed, local = index // edge_tokens, index % edge_tokens
    key_lat = jnp.where(local % WIN >= place_ref[:, :1], -1000 * first, height // WIN - 1000 * last)
    key_lon = jnp.where(local // WIN >= place_ref[:, 1:], 1 - mixed, mixed)
    late_bias_ref[...] = shifted_bias(shape, place_ref, key_lat, key_lon)


def corner_kernel(shape, corner_ref, qkv_ref, corner_pairs_ref):
    members, height, breadth, channels = shape
    corner = per_member(dot(corner_ref[...], qkv_ref[:, channels:]), members, breadth)
    for member in range(members):
        corner_pairs_ref[member] = corner[member]


def shift_kernel(
    shape, stream_ref, queries_ref, mixed_ref, top_ref, total_ref, across, bias_ref, corner, out_ref, up_ref,
    down_ref, updated_ref, attended, turned,
):
    members, height, breadth, channels = shape
    rows = members * height
    bias = bias_ref[...]
    for member in range(members):
        key, value = (
            jnp.concatenate(
                [block[member, :, i * channels : (i + 1) * channels] for block in (across, corner)], axis=0
            )
            for i in range(2)
        )
        late = partial_attention(queries_ref[member], key, value, bias)
        early = mixed_ref[member], top_ref[member], total_ref[member]
        attended[:, member * height : (member + 1) * height, :] = (
            joined_attention(early, late).astype(bf16).reshape(breadth, height, channels)
        )
    stream = stream_ref[...] + dot(attended[...].reshape(breadth * rows, channels), out_ref[...])
    stream = feed_forward(stream, up_ref, down_ref)
    for column in range(breadth):
        for part in range(channels // LANES):
            turned[part, pl.ds(column, rows, stride=breadth), :] = stream[
                column * rows : (column + 1) * rows, part * LANES : (part + 1) * LANES
            ]
    for part in range(channels // LANES):
        updated_ref[:, part * LANES : (part + 1) * LANES] = turned[part].astype(bf16)


def in_vmem(count):
    return [pl.BlockSpec(memory_space=pltpu.VMEM)] * count


def per_device(
    fields, land_mask, offsets, land_embed, win_qkv, win_out, win_up, win_down, mem_qkv, mem_out,
    shift_qkv, shift_out, shift_up, shift_down,
):
    shape = fields.shape
    members, height, breadth, channels = shape
    rows, tokens = members * height, members * height * breadth
    edge_tokens = members * WIN * breadth
    params = pltpu.CompilerParams(vmem_limit_bytes=VMEM_LIMIT)
    sources = (
        fields.reshape(tokens, channels), land_mask.T, land_embed.reshape(1, channels),
        win_qkv, win_out, win_up, win_down,
    )
    stream, normed = pl.pallas_call(
        functools.partial(window_kernel, shape),
        out_shape=(
            jax.ShapeDtypeStruct((tokens, channels), f32),
            jax.ShapeDtypeStruct((tokens, channels), bf16),
        ),
        in_specs=[pl.BlockSpec(memory_space=pltpu.HBM)] * len(sources),
        out_specs=tuple(in_vmem(2)),
        scratch_shapes=[pltpu.VMEM(source.shape, source.dtype) for source in sources]
        + [
            pltpu.SemaphoreType.DMA((len(sources),)),
            pltpu.VMEM((channels // LANES, tokens, LANES), f32),
            pltpu.VMEM((breadth, rows, 3 * channels), bf16),
            pltpu.VMEM((breadth, rows, channels), bf16),
        ],
        compiler_params=pltpu.CompilerParams(vmem_limit_bytes=60 * 1024 * 1024),
    )(*sources)

    groups = lax.axis_size("member")
    blocks = [normed]
    bit = 1
    while bit * 2 < groups:
        bit *= 2
    far = [lax.ppermute(normed, "member", [(i, i ^ bit) for i in range(groups)])]
    partners = []
    while bit > 1:
        bit //= 2
        partners.append([(i, i ^ bit) for i in range(groups)])

    def spread(blocks):
        for partner in partners:
            blocks = blocks + [lax.ppermute(block, "member", partner) for block in blocks]
        return blocks

    near = spread([normed])
    part_shape = jax.ShapeDtypeStruct((breadth, rows, channels), f32)
    queries, *parts = pl.pallas_call(
        functools.partial(near_kernel, shape),
        out_shape=(jax.ShapeDtypeStruct((breadth, rows, channels), bf16),) + (part_shape,) * 3,
        in_specs=in_vmem(1 + len(near)),
        out_specs=tuple(in_vmem(4)),
        scratch_shapes=[pltpu.VMEM((breadth, rows * len(near), 2 * channels), bf16)],
        compiler_params=params,
    )(*near, mem_qkv)
    branch = offsets[1] - 1
    far[0], branch, queries, *parts = lax.optimization_barrier((far[0], branch, queries, *parts))
    far = spread(far)

    lat_count, lon_count = lax.axis_size("lat"), lax.axis_size("lon")
    lat_index = lax.axis_index("lat")
    down = [(i, i + 1) for i in range(lat_count - 1)]
    up = [(b, a) for a, b in down]
    lat_pairs = [down + up] if lat_count == 2 else [down, up]
    late, normed, *edges = pl.pallas_call(
        functools.partial(member_kernel, shape, lat_count),
        out_shape=(
            jax.ShapeDtypeStruct((tokens, channels), f32),
            jax.ShapeDtypeStruct((tokens, channels), bf16),
        )
        + (jax.ShapeDtypeStruct((edge_tokens, channels), bf16),) * len(lat_pairs),
        in_specs=in_vmem(7 + len(far)),
        out_specs=tuple(in_vmem(2 + len(lat_pairs))),
        scratch_shapes=[
            pltpu.VMEM((breadth, rows * len(far), 2 * channels), bf16),
            pltpu.VMEM((breadth, rows, channels), bf16),
        ],
        compiler_params=params,
    )(stream, queries, *parts, *far, mem_qkv, mem_out)

    ring = [(i, (i + 1) % lon_count) for i in range(lon_count)]
    back = [(b, a) for a, b in ring]

    def gather(amount, own, *edges):
        low = lax.ppermute(own[amount:], "lon", ring)
        high = lax.ppermute(own[:amount], "lon", back)
        straight = [lax.ppermute(edge, "lat", pairs) for edge, pairs in zip(edges, lat_pairs)]
        end_shape = jax.ShapeDtypeStruct((edge_tokens, channels), bf16)
        side, *ends = pl.pallas_call(
            functools.partial(join_kernel, shape, lat_count, amount),
            out_shape=(jax.ShapeDtypeStruct((breadth, rows, channels), bf16),)
            + (end_shape,) * len(lat_pairs),
            in_specs=in_vmem(2),
            out_specs=tuple(in_vmem(1 + len(lat_pairs))),
            compiler_params=params,
        )(*((high, low) if 2 * amount <= breadth else (low, high)))
        corners = [lax.ppermute(end, "lat", pairs) for end, pairs in zip(ends, lat_pairs)]
        if lat_count == 2:
            edge, corner = straight[0], corners[0]
        else:
            above = jnp.tile(jnp.arange(WIN, dtype=jnp.int32) >= offsets[0], breadth * members)[:, None]
            edge, corner = jnp.where(above, *straight), jnp.where(above, *corners)

        pairs_shape = jax.ShapeDtypeStruct((members, breadth * WIN, 2 * channels), bf16)
        corner = pl.pallas_call(
            functools.partial(corner_kernel, shape),
            out_shape=pairs_shape,
            in_specs=in_vmem(2),
            out_specs=in_vmem(1)[0],
            compiler_params=params,
        )(corner, shift_qkv)
        bias_shape = jax.ShapeDtypeStruct((breadth * height, 2 * breadth * WIN), f32)
        whole_shape = (members, breadth * height, channels)
        return pl.pallas_call(
            functools.partial(early_kernel, shape, lat_count),
            out_shape=(jax.ShapeDtypeStruct(whole_shape, bf16),)
            + (jax.ShapeDtypeStruct(whole_shape, f32),) * 3
            + (pairs_shape, bias_shape),
            in_specs=in_vmem(5),
            out_specs=tuple(in_vmem(6)),
            scratch_shapes=[
                pltpu.VMEM((breadth, rows, 3 * channels), bf16),
                pltpu.VMEM((breadth, rows, 2 * channels), bf16),
            ],
            compiler_params=params,
        )(offsets.reshape(1, -1), own.reshape(tokens, channels), side.reshape(tokens, channels), edge, shift_qkv) + (
            corner,
        )

    *early, corner = lax.switch(
        branch,
        [functools.partial(gather, amount) for amount in range(1, WIN)],
        normed.reshape(breadth, rows, channels), *edges,
    )
    updated = pl.pallas_call(
        functools.partial(shift_kernel, shape),
        out_shape=jax.ShapeDtypeStruct((tokens, channels), bf16),
        in_specs=in_vmem(11),
        out_specs=pl.BlockSpec(memory_space=pltpu.VMEM),
        scratch_shapes=[
            pltpu.VMEM((breadth, rows, channels), bf16),
            pltpu.VMEM((channels // LANES, tokens, LANES), f32),
        ],
        compiler_params=params,
    )(late, *early, corner, shift_out, shift_up, shift_down)
    return updated.reshape(shape)


def solution(mesh):
    return jax.shard_map(
        per_device,
        mesh=mesh,
        in_specs=(P("member", "lat", "lon", None), P("lat", "lon")) + (P(),) * 12,
        out_specs=P("member", "lat", "lon", None),
        check_vma=False,
    )
```

```python
import functools

import jax
import jax.numpy as jnp
from jax import lax
from jax.experimental import pallas as pl
from jax.experimental.pallas import tpu as pltpu
from jax.sharding import PartitionSpec as P

HEADS = 4
WIN = 8
LANES = 128
EPSILON = 1e-05
MASKED = -1e30
VMEM_LIMIT = 40 * 1024 * 1024

f32 = jnp.float32
bf16 = jnp.bfloat16


def normalize(stream):
    average = jnp.mean(stream, axis=-1, keepdims=True)
    centered = stream - average
    spread = jnp.mean(centered * centered, axis=-1, keepdims=True)
    return (centered * lax.rsqrt(spread + EPSILON)).astype(bf16)


def dot(a, b):
    return jnp.dot(a, b, preferred_element_type=f32)


def head_lanes(channels):
    return lax.broadcasted_iota(jnp.int32, (1, channels), 1) // (channels // HEADS)


def partial_attention(query, key, value, bias):
    amount, channels = query.shape
    lanes = head_lanes(channels)
    scale = (channels // HEADS) ** (-0.5)
    stacked = jnp.concatenate(
        [query * jnp.where(lanes == head, scale, 0.0).astype(bf16) for head in range(HEADS)], axis=0
    )
    scores = lax.dot_general(stacked, key, (((1,), (1,)), ((), ())), preferred_element_type=f32)
    scores = scores.reshape(HEADS, amount, key.shape[0]) + bias[None]
    top = jnp.max(scores, axis=-1, keepdims=True)
    powers = jnp.exp(scores - top)
    total = jnp.sum(powers, axis=-1, keepdims=True)
    mixed = dot(powers.astype(bf16).reshape(HEADS * amount, key.shape[0]), value)

    def in_lanes(parts):
        result = parts[0]
        for head in range(1, HEADS):
            result = jnp.where(lanes == head, parts[head], result)
        return jnp.broadcast_to(result, (amount, channels))

    return in_lanes(mixed.reshape(HEADS, amount, channels)), in_lanes(top), in_lanes(total)


def joined_attention(one, two):
    top = jnp.maximum(one[1], two[1])
    first, second = jnp.exp(one[1] - top), jnp.exp(two[1] - top)
    return (first * one[0] + second * two[0]) / (first * one[2] + second * two[2])


def attend(query, key, value, bias):
    mixed, _, total = partial_attention(query, key, value, bias)
    return (mixed / total).astype(bf16)


def feed_forward(stream, up_ref, down_ref, chunk=256):
    normed = normalize(stream)
    total = stream
    for start in range(0, up_ref.shape[1], chunk):
        raw = dot(normed, up_ref[:, start : start + chunk])
        hidden = (0.5 * raw * (1.0 + lax.erf(raw * 0.5**0.5))).astype(bf16)
        total = total + dot(hidden, down_ref[start : start + chunk, :])
    return total


def window_kernel(
    shape, *refs
):
    members, height, breadth, channels = shape
    sources, refs = refs[:7], refs[7:]
    stream_ref, normed_ref, *places, semaphores, turned, held, attended = refs
    copies = [
        pltpu.make_async_copy(source, place, semaphores.at[index])
        for index, (source, place) in enumerate(zip(sources, places))
    ]
    for copy in copies:
        copy.start()
    fields_ref, land_ref, embed_ref, qkv_ref, out_ref, up_ref, down_ref = places
    rows = members * height
    for copy in copies[:3]:
        copy.wait()
    for part in range(channels // LANES):
        turned[part] = fields_ref[:, part * LANES : (part + 1) * LANES].astype(f32)
    same = lax.broadcasted_iota(jnp.int32, (1, height, height), 1) == lax.broadcasted_iota(
        jnp.int32, (1, height, height), 2
    )
    land = jnp.sum(
        jnp.where(same, land_ref[...].astype(f32)[:, None, :], 0.0), axis=-1, keepdims=True
    )
    columns = []
    for column in range(breadth):
        taken = jnp.concatenate(
            [turned[part, pl.ds(column, rows, stride=breadth), :] for part in range(channels // LANES)],
            axis=1,
        ).reshape(members, height, channels)
        columns.append((taken + (land[column] * embed_ref[...])[None]).reshape(rows, channels))
    stream = jnp.concatenate(columns, axis=0)
    normed = normalize(stream)
    copies[3].wait()
    held[...] = dot(normed, qkv_ref[...]).astype(bf16).reshape(breadth, rows, 3 * channels)
    tokens = breadth * height
    block = (lax.broadcasted_iota(jnp.int32, (tokens, tokens), 0) % height) // WIN
    other = (lax.broadcasted_iota(jnp.int32, (tokens, tokens), 1) % height) // WIN
    bias = jnp.where(block == other, 0.0, MASKED).astype(f32)
    for member in range(members):
        part = slice(member * height, (member + 1) * height)
        query, key, value = (
            held[:, part, i * channels : (i + 1) * channels].reshape(tokens, channels) for i in range(3)
        )
        attended[:, part, :] = attend(query, key, value, bias).reshape(breadth, height, channels)
    for copy in copies[4:]:
        copy.wait()
    stream = stream + dot(attended[...].reshape(breadth * rows, channels), out_ref[...])
    stream = feed_forward(stream, up_ref, down_ref)
    stream_ref[...] = stream
    normed_ref[...] = normalize(stream)


def member_pairs(shape, block_refs, qkv_ref, pairs):
    members, height, breadth, channels = shape
    rows = members * height
    for index, block_ref in enumerate(block_refs):
        pairs[:, index * rows : (index + 1) * rows, :] = (
            dot(block_ref[...], qkv_ref[:, channels:]).astype(bf16).reshape(breadth, rows, 2 * channels)
        )
    amount = pairs.shape[1]
    row = lax.broadcasted_iota(jnp.int32, (rows, amount), 0) % height
    other = lax.broadcasted_iota(jnp.int32, (rows, amount), 1) % height
    return jnp.where(row == other, 0.0, MASKED).astype(f32)


def near_kernel(shape, *refs):
    members, height, breadth, channels = shape
    *block_refs, qkv_ref, queries_ref, mixed_ref, top_ref, total_ref, pairs = refs
    rows = members * height
    queries_ref[...] = (
        dot(block_refs[0][...], qkv_ref[:, :channels]).astype(bf16).reshape(breadth, rows, channels)
    )
    bias = member_pairs(shape, block_refs, qkv_ref, pairs)
    for column in range(breadth):
        mixed_ref[column], top_ref[column], total_ref[column] = partial_attention(
            queries_ref[column], pairs[column, :, :channels], pairs[column, :, channels:], bias
        )


def member_kernel(shape, lat_count, stream_ref, queries_ref, mixed_ref, top_ref, total_ref, *refs):
    members, height, breadth, channels = shape
    sides = 1 if lat_count == 2 else 2
    *block_refs, qkv_ref, out_ref = refs[: -4 - sides]
    late_ref, normed_ref, *edge_refs = refs[-4 - sides : -2]
    pairs, attended = refs[-2:]
    rows = members * height
    bias = member_pairs(shape, block_refs, qkv_ref, pairs)
    for column in range(breadth):
        far = partial_attention(
            queries_ref[column], pairs[column, :, :channels], pairs[column, :, channels:], bias
        )
        near = mixed_ref[column], top_ref[column], total_ref[column]
        attended[column] = joined_attention(near, far).astype(bf16)
    stream = stream_ref[...] + dot(attended[...].reshape(breadth * rows, channels), out_ref[...])
    late_ref[...] = stream
    normed = normalize(stream)
    normed_ref[...] = normed
    lines = normed.astype(f32).reshape(breadth * members, height, channels)
    for edge_ref, edge in zip(edge_refs, lat_ends(lines, lat_count)):
        edge_ref[...] = edge.reshape(breadth * members * WIN, channels).astype(bf16)


def per_member(lines, members, breadth):
    lines = lines.reshape(breadth, members * WIN, lines.shape[-1])
    return [
        lines[:, member * WIN : (member + 1) * WIN].reshape(breadth * WIN, lines.shape[-1]).astype(bf16)
        for member in range(members)
    ]


def join_kernel(breadth, amount, first_ref, second_ref, side_ref):
    high_ref, low_ref = (first_ref, second_ref) if 2 * amount <= breadth else (second_ref, first_ref)
    side_ref[:amount] = high_ref[...]
    side_ref[amount:] = low_ref[...]


def lat_ends(lines, lat_count):
    top, bottom = lines[:, :WIN], lines[:, lines.shape[1] - WIN :]
    if lat_count == 2:
        return [jnp.where(lax.axis_index("lat") == 0, bottom, top)]
    return [bottom, top]


def lat_window(row, place_ref):
    return (row - place_ref[:, :1] + WIN) // WIN


def shifted_bias(shape, place_ref, key_lat, key_lon):
    members, height, breadth, channels = shape
    index = lax.broadcasted_iota(jnp.int32, (breadth * height, 1), 0)
    query_lon = jnp.where(index // height >= place_ref[:, 1:], 1, 0)
    query_tag = 2 * lat_window(index % height, place_ref) + query_lon
    return jnp.where(query_tag == 2 * key_lat + key_lon, 0.0, MASKED).astype(f32)


def early_kernel(
    shape, lat_count, place_ref, normed_ref, side_ref, qkv_ref,
    queries_ref, mixed_ref, top_ref, total_ref, late_bias_ref, held, beside,
):
    members, height, breadth, channels = shape
    rows, tokens = members * height, breadth * height
    held[...] = dot(normed_ref[...], qkv_ref[...]).astype(bf16).reshape(breadth, rows, 3 * channels)
    beside[...] = dot(side_ref[...], qkv_ref[:, channels:]).astype(bf16).reshape(
        breadth, rows, 2 * channels
    )
    index = lax.broadcasted_iota(jnp.int32, (1, 2 * tokens), 1)
    mixed, local = index // tokens, index % tokens
    key_lon = jnp.where(local // height >= place_ref[:, 1:], 1 - mixed, mixed)
    bias = shifted_bias(shape, place_ref, lat_window(local % height, place_ref), key_lon)
    for member in range(members):
        part = slice(member * height, (member + 1) * height)
        query = held[:, part, :channels].reshape(tokens, channels)
        queries_ref[member] = query
        key, value = (
            jnp.concatenate(
                [
                    held[:, part, (i + 1) * channels : (i + 2) * channels].reshape(tokens, channels),
                    beside[:, part, i * channels : (i + 1) * channels].reshape(tokens, channels),
                ],
                axis=0,
            )
            for i in range(2)
        )
        mixed_ref[member], top_ref[member], total_ref[member] = partial_attention(query, key, value, bias)

    edge_tokens = breadth * WIN
    first = jnp.where(lax.axis_index("lat") == 0, 1, 0)
    last = jnp.where(lax.axis_index("lat") == lat_count - 1, 1, 0)
    index = lax.broadcasted_iota(jnp.int32, (1, 2 * edge_tokens), 1)
    mixed, local = index // edge_tokens, index % edge_tokens
    key_lat = jnp.where(local % WIN >= place_ref[:, :1], -1000 * first, height // WIN - 1000 * last)
    key_lon = jnp.where(local // WIN >= place_ref[:, 1:], 1 - mixed, mixed)
    late_bias_ref[...] = shifted_bias(shape, place_ref, key_lat, key_lon)


def rim_kernel(shape, amount, high_ref, low_ref, edge_ref, qkv_ref, across_ref, corner_ref):
    members, height, breadth, channels = shape
    edge = per_member(dot(edge_ref[...], qkv_ref[:, channels:]), members, breadth)
    high, low = (dot(ref[...], qkv_ref[:, channels:]) for ref in (high_ref, low_ref))
    sides = [high[: members * WIN * amount], low]
    corner = per_member(jnp.concatenate(sides, axis=0), members, breadth)
    for member in range(members):
        across_ref[member] = edge[member]
        corner_ref[member] = corner[member]


def shift_kernel(
    shape, stream_ref, queries_ref, mixed_ref, top_ref, total_ref, bias_ref, across, corner, out_ref, up_ref,
    down_ref, updated_ref, attended, turned,
):
    members, height, breadth, channels = shape
    rows = members * height
    bias = bias_ref[...]
    for member in range(members):
        key, value = (
            jnp.concatenate(
                [block[member, :, i * channels : (i + 1) * channels] for block in (across, corner)], axis=0
            )
            for i in range(2)
        )
        late = partial_attention(queries_ref[member], key, value, bias)
        early = mixed_ref[member], top_ref[member], total_ref[member]
        attended[:, member * height : (member + 1) * height, :] = (
            joined_attention(early, late).astype(bf16).reshape(breadth, height, channels)
        )
    stream = stream_ref[...] + dot(attended[...].reshape(breadth * rows, channels), out_ref[...])
    stream = feed_forward(stream, up_ref, down_ref)
    for column in range(breadth):
        for part in range(channels // LANES):
            turned[part, pl.ds(column, rows, stride=breadth), :] = stream[
                column * rows : (column + 1) * rows, part * LANES : (part + 1) * LANES
            ]
    for part in range(channels // LANES):
        updated_ref[:, part * LANES : (part + 1) * LANES] = turned[part].astype(bf16)


def in_vmem(count):
    return [pl.BlockSpec(memory_space=pltpu.VMEM)] * count


def per_device(
    fields, land_mask, offsets, land_embed, win_qkv, win_out, win_up, win_down, mem_qkv, mem_out,
    shift_qkv, shift_out, shift_up, shift_down,
):
    shape = fields.shape
    members, height, breadth, channels = shape
    rows, tokens = members * height, members * height * breadth
    edge_tokens = members * WIN * breadth
    params = pltpu.CompilerParams(vmem_limit_bytes=VMEM_LIMIT)
    sources = (
        fields.reshape(tokens, channels), land_mask.T, land_embed.reshape(1, channels),
        win_qkv, win_out, win_up, win_down,
    )
    stream, normed = pl.pallas_call(
        functools.partial(window_kernel, shape),
        out_shape=(
            jax.ShapeDtypeStruct((tokens, channels), f32),
            jax.ShapeDtypeStruct((tokens, channels), bf16),
        ),
        in_specs=[pl.BlockSpec(memory_space=pltpu.HBM)] * len(sources),
        out_specs=tuple(in_vmem(2)),
        scratch_shapes=[pltpu.VMEM(source.shape, source.dtype) for source in sources]
        + [
            pltpu.SemaphoreType.DMA((len(sources),)),
            pltpu.VMEM((channels // LANES, tokens, LANES), f32),
            pltpu.VMEM((breadth, rows, 3 * channels), bf16),
            pltpu.VMEM((breadth, rows, channels), bf16),
        ],
        compiler_params=pltpu.CompilerParams(vmem_limit_bytes=60 * 1024 * 1024),
    )(*sources)

    groups = lax.axis_size("member")
    blocks = [normed]
    bit = 1
    while bit * 2 < groups:
        bit *= 2
    far = [lax.ppermute(normed, "member", [(i, i ^ bit) for i in range(groups)])]
    partners = []
    while bit > 1:
        bit //= 2
        partners.append([(i, i ^ bit) for i in range(groups)])

    def spread(blocks):
        for partner in partners:
            blocks = blocks + [lax.ppermute(block, "member", partner) for block in blocks]
        return blocks

    near = spread([normed])
    part_shape = jax.ShapeDtypeStruct((breadth, rows, channels), f32)
    queries, *parts = pl.pallas_call(
        functools.partial(near_kernel, shape),
        out_shape=(jax.ShapeDtypeStruct((breadth, rows, channels), bf16),) + (part_shape,) * 3,
        in_specs=in_vmem(1 + len(near)),
        out_specs=tuple(in_vmem(4)),
        scratch_shapes=[pltpu.VMEM((breadth, rows * len(near), 2 * channels), bf16)],
        compiler_params=params,
    )(*near, mem_qkv)
    branch = offsets[1] - 1
    far[0], branch, queries, *parts = lax.optimization_barrier((far[0], branch, queries, *parts))
    far = spread(far)

    lat_count, lon_count = lax.axis_size("lat"), lax.axis_size("lon")
    lat_index = lax.axis_index("lat")
    down = [(i, i + 1) for i in range(lat_count - 1)]
    up = [(b, a) for a, b in down]
    lat_pairs = [down + up] if lat_count == 2 else [down, up]
    late, normed, *edges = pl.pallas_call(
        functools.partial(member_kernel, shape, lat_count),
        out_shape=(
            jax.ShapeDtypeStruct((tokens, channels), f32),
            jax.ShapeDtypeStruct((tokens, channels), bf16),
        )
        + (jax.ShapeDtypeStruct((edge_tokens, channels), bf16),) * len(lat_pairs),
        in_specs=in_vmem(7 + len(far)),
        out_specs=tuple(in_vmem(2 + len(lat_pairs))),
        scratch_shapes=[
            pltpu.VMEM((breadth, rows * len(far), 2 * channels), bf16),
            pltpu.VMEM((breadth, rows, channels), bf16),
        ],
        compiler_params=params,
    )(stream, queries, *parts, *far, mem_qkv, mem_out)

    ring = [(i, (i + 1) % lon_count) for i in range(lon_count)]
    back = [(b, a) for a, b in ring]

    def gather(amount, own, *edges):
        low = lax.ppermute(own[amount:], "lon", ring)
        high = lax.ppermute(own[:amount], "lon", back)

        def diagonal(block, lat_pairs, lon_pairs):
            pairs = [
                (a * lon_count + c, b * lon_count + d) for a, b in lat_pairs for c, d in lon_pairs
            ]
            return lax.ppermute(block, ("lat", "lon"), pairs)

        lines = members * WIN * amount
        low_corners = [diagonal(edge[lines:], pairs, ring) for edge, pairs in zip(edges, lat_pairs)]
        longer = amount
        if 2 * amount > breadth:
            longer = min(breadth, max(amount, 2 * (breadth - amount) + 1))
        some = members * WIN * longer
        high_corners = [diagonal(edge[:some], pairs, back) for edge, pairs in zip(edges, lat_pairs)]
        straight = [lax.ppermute(edge, "lat", pairs) for edge, pairs in zip(edges, lat_pairs)]
        if lat_count > 2:
            above = jnp.tile(jnp.arange(WIN, dtype=jnp.int32) >= offsets[0], breadth * members)[:, None]
            straight = [jnp.where(above, *straight)]
            low_corners = [jnp.where(above[lines:], *low_corners)]
            high_corners = [jnp.where(above[:some], *high_corners)]
        side = pl.pallas_call(
            functools.partial(join_kernel, breadth, amount),
            out_shape=jax.ShapeDtypeStruct((breadth, rows, channels), bf16),
            in_specs=in_vmem(2),
            out_specs=in_vmem(1)[0],
            compiler_params=params,
        )(*((high, low) if 2 * amount <= breadth else (low, high)))
        whole_shape = (members, breadth * height, channels)
        early = pl.pallas_call(
            functools.partial(early_kernel, shape, lat_count),
            out_shape=(jax.ShapeDtypeStruct(whole_shape, bf16),)
            + (jax.ShapeDtypeStruct(whole_shape, f32),) * 3
            + (jax.ShapeDtypeStruct((breadth * height, 2 * breadth * WIN), f32),),
            in_specs=in_vmem(4),
            out_specs=tuple(in_vmem(5)),
            scratch_shapes=[
                pltpu.VMEM((breadth, rows, 3 * channels), bf16),
                pltpu.VMEM((breadth, rows, 2 * channels), bf16),
            ],
            compiler_params=params,
        )(offsets.reshape(1, -1), own.reshape(tokens, channels), side.reshape(tokens, channels), shift_qkv)
        rim = high_corners[0], low_corners[0], straight[0]
        *rim, first = lax.optimization_barrier((*rim, early[0]))
        early = (first,) + tuple(early[1:])
        across, corner = pl.pallas_call(
            functools.partial(rim_kernel, shape, amount),
            out_shape=(jax.ShapeDtypeStruct((members, breadth * WIN, 2 * channels), bf16),) * 2,
            in_specs=in_vmem(4),
            out_specs=tuple(in_vmem(2)),
            compiler_params=params,
        )(*rim, shift_qkv)
        return early + (across, corner)

    *early, across, corner = lax.switch(
        branch,
        [functools.partial(gather, amount) for amount in range(1, WIN)],
        normed.reshape(breadth, rows, channels), *edges,
    )
    updated = pl.pallas_call(
        functools.partial(shift_kernel, shape),
        out_shape=jax.ShapeDtypeStruct((tokens, channels), bf16),
        in_specs=in_vmem(11),
        out_specs=pl.BlockSpec(memory_space=pltpu.VMEM),
        scratch_shapes=[
            pltpu.VMEM((breadth, rows, channels), bf16),
            pltpu.VMEM((channels // LANES, tokens, LANES), f32),
        ],
        compiler_params=params,
    )(late, *early, across, corner, shift_out, shift_up, shift_down)
    return updated.reshape(shape)


def solution(mesh):
    return jax.shard_map(
        per_device,
        mesh=mesh,
        in_specs=(P("member", "lat", "lon", None), P("lat", "lon")) + (P(),) * 12,
        out_specs=P("member", "lat", "lon", None),
        check_vma=False,
    )
```

```python
import functools

import jax
import jax.numpy as jnp
from jax import lax
from jax.experimental import pallas as pl
from jax.experimental.pallas import tpu as pltpu
from jax.sharding import PartitionSpec as P

HEADS = 4
WIN = 8
LANES = 128
EPSILON = 1e-05
MASKED = -1e30
VMEM_LIMIT = 40 * 1024 * 1024

f32 = jnp.float32
bf16 = jnp.bfloat16


def normalize(stream):
    average = jnp.mean(stream, axis=-1, keepdims=True)
    centered = stream - average
    spread = jnp.mean(centered * centered, axis=-1, keepdims=True)
    return (centered * lax.rsqrt(spread + EPSILON)).astype(bf16)


def dot(a, b):
    return jnp.dot(a, b, preferred_element_type=f32)


def head_lanes(channels):
    return lax.broadcasted_iota(jnp.int32, (1, channels), 1) // (channels // HEADS)


def partial_attention(query, key, value, bias):
    amount, channels = query.shape
    lanes = head_lanes(channels)
    scale = (channels // HEADS) ** (-0.5)
    stacked = jnp.concatenate(
        [query * jnp.where(lanes == head, scale, 0.0).astype(bf16) for head in range(HEADS)], axis=0
    )
    scores = lax.dot_general(stacked, key, (((1,), (1,)), ((), ())), preferred_element_type=f32)
    scores = scores.reshape(HEADS, amount, key.shape[0]) + bias[None]
    top = jnp.max(scores, axis=-1, keepdims=True)
    powers = jnp.exp(scores - top)
    total = jnp.sum(powers, axis=-1, keepdims=True)
    mixed = dot(powers.astype(bf16).reshape(HEADS * amount, key.shape[0]), value)

    def in_lanes(parts):
        result = parts[0]
        for head in range(1, HEADS):
            result = jnp.where(lanes == head, parts[head], result)
        return jnp.broadcast_to(result, (amount, channels))

    return in_lanes(mixed.reshape(HEADS, amount, channels)), in_lanes(top), in_lanes(total)


def joined_attention(one, two):
    top = jnp.maximum(one[1], two[1])
    first, second = jnp.exp(one[1] - top), jnp.exp(two[1] - top)
    return (first * one[0] + second * two[0]) / (first * one[2] + second * two[2])


def attend(query, key, value, bias):
    mixed, _, total = partial_attention(query, key, value, bias)
    return (mixed / total).astype(bf16)


def feed_forward(stream, up_ref, down_ref, chunk=256):
    normed = normalize(stream)
    total = stream
    for start in range(0, up_ref.shape[1], chunk):
        raw = dot(normed, up_ref[:, start : start + chunk])
        hidden = (0.5 * raw * (1.0 + lax.erf(raw * 0.5**0.5))).astype(bf16)
        total = total + dot(hidden, down_ref[start : start + chunk, :])
    return total


def window_kernel(
    shape, *refs
):
    members, height, breadth, channels = shape
    sources, refs = refs[:7], refs[7:]
    stream_ref, normed_ref, *places, semaphores, turned, held, attended = refs
    copies = [
        pltpu.make_async_copy(source, place, semaphores.at[index])
        for index, (source, place) in enumerate(zip(sources, places))
    ]
    for copy in copies:
        copy.start()
    fields_ref, land_ref, embed_ref, qkv_ref, out_ref, up_ref, down_ref = places
    rows = members * height
    for copy in copies[:3]:
        copy.wait()
    for part in range(channels // LANES):
        turned[part] = fields_ref[:, part * LANES : (part + 1) * LANES].astype(f32)
    same = lax.broadcasted_iota(jnp.int32, (1, height, height), 1) == lax.broadcasted_iota(
        jnp.int32, (1, height, height), 2
    )
    land = jnp.sum(
        jnp.where(same, land_ref[...].astype(f32)[:, None, :], 0.0), axis=-1, keepdims=True
    )
    columns = []
    for column in range(breadth):
        taken = jnp.concatenate(
            [turned[part, pl.ds(column, rows, stride=breadth), :] for part in range(channels // LANES)],
            axis=1,
        ).reshape(members, height, channels)
        columns.append((taken + (land[column] * embed_ref[...])[None]).reshape(rows, channels))
    stream = jnp.concatenate(columns, axis=0)
    normed = normalize(stream)
    copies[3].wait()
    held[...] = dot(normed, qkv_ref[...]).astype(bf16).reshape(breadth, rows, 3 * channels)
    tokens = breadth * height
    block = (lax.broadcasted_iota(jnp.int32, (tokens, tokens), 0) % height) // WIN
    other = (lax.broadcasted_iota(jnp.int32, (tokens, tokens), 1) % height) // WIN
    bias = jnp.where(block == other, 0.0, MASKED).astype(f32)
    for member in range(members):
        part = slice(member * height, (member + 1) * height)
        query, key, value = (
            held[:, part, i * channels : (i + 1) * channels].reshape(tokens, channels) for i in range(3)
        )
        attended[:, part, :] = attend(query, key, value, bias).reshape(breadth, height, channels)
    for copy in copies[4:]:
        copy.wait()
    stream = stream + dot(attended[...].reshape(breadth * rows, channels), out_ref[...])
    stream = feed_forward(stream, up_ref, down_ref)
    stream_ref[...] = stream
    normed_ref[...] = normalize(stream)


def member_pairs(shape, block_refs, qkv_ref, pairs):
    members, height, breadth, channels = shape
    rows = members * height
    for index, block_ref in enumerate(block_refs):
        pairs[:, index * rows : (index + 1) * rows, :] = (
            dot(block_ref[...], qkv_ref[:, channels:]).astype(bf16).reshape(breadth, rows, 2 * channels)
        )
    amount = pairs.shape[1]
    row = lax.broadcasted_iota(jnp.int32, (rows, amount), 0) % height
    other = lax.broadcasted_iota(jnp.int32, (rows, amount), 1) % height
    return jnp.where(row == other, 0.0, MASKED).astype(f32)


def near_kernel(shape, *refs):
    members, height, breadth, channels = shape
    *block_refs, qkv_ref, queries_ref, mixed_ref, top_ref, total_ref, pairs = refs
    rows = members * height
    queries_ref[...] = (
        dot(block_refs[0][...], qkv_ref[:, :channels]).astype(bf16).reshape(breadth, rows, channels)
    )
    bias = member_pairs(shape, block_refs, qkv_ref, pairs)
    for column in range(breadth):
        mixed_ref[column], top_ref[column], total_ref[column] = partial_attention(
            queries_ref[column], pairs[column, :, :channels], pairs[column, :, channels:], bias
        )


def member_kernel(shape, lat_count, stream_ref, queries_ref, mixed_ref, top_ref, total_ref, *refs):
    members, height, breadth, channels = shape
    sides = 1 if lat_count == 2 else 2
    *block_refs, qkv_ref, out_ref = refs[: -4 - sides]
    late_ref, normed_ref, *edge_refs = refs[-4 - sides : -2]
    pairs, attended = refs[-2:]
    rows = members * height
    bias = member_pairs(shape, block_refs, qkv_ref, pairs)
    for column in range(breadth):
        far = partial_attention(
            queries_ref[column], pairs[column, :, :channels], pairs[column, :, channels:], bias
        )
        near = mixed_ref[column], top_ref[column], total_ref[column]
        attended[column] = joined_attention(near, far).astype(bf16)
    stream = stream_ref[...] + dot(attended[...].reshape(breadth * rows, channels), out_ref[...])
    late_ref[...] = stream
    normed = normalize(stream)
    normed_ref[...] = normed
    lines = normed.astype(f32).reshape(breadth * members, height, channels)
    for edge_ref, edge in zip(edge_refs, lat_ends(lines, lat_count)):
        edge_ref[...] = edge.reshape(breadth * members * WIN, channels).astype(bf16)


def per_member(lines, members, breadth):
    lines = lines.reshape(breadth, members * WIN, lines.shape[-1])
    return [
        lines[:, member * WIN : (member + 1) * WIN].reshape(breadth * WIN, lines.shape[-1]).astype(bf16)
        for member in range(members)
    ]


def lat_ends(lines, lat_count):
    top, bottom = lines[:, :WIN], lines[:, lines.shape[1] - WIN :]
    if lat_count == 2:
        return [jnp.where(lax.axis_index("lat") == 0, bottom, top)]
    return [bottom, top]


def lat_window(row, place_ref):
    return (row - place_ref[:, :1] + WIN) // WIN


def shifted_bias(shape, place_ref, key_lat, key_lon):
    members, height, breadth, channels = shape
    index = lax.broadcasted_iota(jnp.int32, (breadth * height, 1), 0)
    query_lon = jnp.where(index // height >= place_ref[:, 1:], 1, 0)
    query_tag = 2 * lat_window(index % height, place_ref) + query_lon
    return jnp.where(query_tag == 2 * key_lat + key_lon, 0.0, MASKED).astype(f32)


def early_kernel(
    shape, lat_count, amount, place_ref, normed_ref, high_ref, low_ref, qkv_ref,
    queries_ref, mixed_ref, top_ref, total_ref, late_bias_ref, held, beside,
):
    members, height, breadth, channels = shape
    rows, tokens = members * height, breadth * height
    held[...] = dot(normed_ref[...], qkv_ref[...]).astype(bf16).reshape(breadth, rows, 3 * channels)
    for part, ref in ((slice(0, amount), high_ref), (slice(amount, breadth), low_ref)):
        block = ref[...].reshape(-1, channels)
        beside[part] = dot(block, qkv_ref[:, channels:]).astype(bf16).reshape(-1, rows, 2 * channels)
    index = lax.broadcasted_iota(jnp.int32, (1, 2 * tokens), 1)
    mixed, local = index // tokens, index % tokens
    key_lon = jnp.where(local // height >= place_ref[:, 1:], 1 - mixed, mixed)
    bias = shifted_bias(shape, place_ref, lat_window(local % height, place_ref), key_lon)
    for member in range(members):
        part = slice(member * height, (member + 1) * height)
        query = held[:, part, :channels].reshape(tokens, channels)
        queries_ref[member] = query
        key, value = (
            jnp.concatenate(
                [
                    held[:, part, (i + 1) * channels : (i + 2) * channels].reshape(tokens, channels),
                    beside[:, part, i * channels : (i + 1) * channels].reshape(tokens, channels),
                ],
                axis=0,
            )
            for i in range(2)
        )
        mixed_ref[member], top_ref[member], total_ref[member] = partial_attention(query, key, value, bias)

    edge_tokens = breadth * WIN
    first = jnp.where(lax.axis_index("lat") == 0, 1, 0)
    last = jnp.where(lax.axis_index("lat") == lat_count - 1, 1, 0)
    index = lax.broadcasted_iota(jnp.int32, (1, 2 * edge_tokens), 1)
    mixed, local = index // edge_tokens, index % edge_tokens
    key_lat = jnp.where(local % WIN >= place_ref[:, :1], -1000 * first, height // WIN - 1000 * last)
    key_lon = jnp.where(local // WIN >= place_ref[:, 1:], 1 - mixed, mixed)
    late_bias_ref[...] = shifted_bias(shape, place_ref, key_lat, key_lon)


def rim_kernel(shape, amount, high_ref, low_ref, edge_ref, qkv_ref, across_ref, corner_ref):
    members, height, breadth, channels = shape
    edge = per_member(dot(edge_ref[...], qkv_ref[:, channels:]), members, breadth)
    high, low = (dot(ref[...], qkv_ref[:, channels:]) for ref in (high_ref, low_ref))
    sides = [high[: members * WIN * amount], low]
    corner = per_member(jnp.concatenate(sides, axis=0), members, breadth)
    for member in range(members):
        across_ref[member] = edge[member]
        corner_ref[member] = corner[member]


def shift_kernel(
    shape, stream_ref, queries_ref, mixed_ref, top_ref, total_ref, bias_ref, across, corner, out_ref, up_ref,
    down_ref, updated_ref, attended, turned,
):
    members, height, breadth, channels = shape
    rows = members * height
    bias = bias_ref[...]
    for member in range(members):
        key, value = (
            jnp.concatenate(
                [block[member, :, i * channels : (i + 1) * channels] for block in (across, corner)], axis=0
            )
            for i in range(2)
        )
        late = partial_attention(queries_ref[member], key, value, bias)
        early = mixed_ref[member], top_ref[member], total_ref[member]
        attended[:, member * height : (member + 1) * height, :] = (
            joined_attention(early, late).astype(bf16).reshape(breadth, height, channels)
        )
    stream = stream_ref[...] + dot(attended[...].reshape(breadth * rows, channels), out_ref[...])
    stream = feed_forward(stream, up_ref, down_ref)
    for column in range(breadth):
        for part in range(channels // LANES):
            turned[part, pl.ds(column, rows, stride=breadth), :] = stream[
                column * rows : (column + 1) * rows, part * LANES : (part + 1) * LANES
            ]
    for part in range(channels // LANES):
        updated_ref[:, part * LANES : (part + 1) * LANES] = turned[part].astype(bf16)


def in_vmem(count):
    return [pl.BlockSpec(memory_space=pltpu.VMEM)] * count


def per_device(
    fields, land_mask, offsets, land_embed, win_qkv, win_out, win_up, win_down, mem_qkv, mem_out,
    shift_qkv, shift_out, shift_up, shift_down,
):
    shape = fields.shape
    members, height, breadth, channels = shape
    rows, tokens = members * height, members * height * breadth
    edge_tokens = members * WIN * breadth
    params = pltpu.CompilerParams(vmem_limit_bytes=VMEM_LIMIT)
    sources = (
        fields.reshape(tokens, channels), land_mask.T, land_embed.reshape(1, channels),
        win_qkv, win_out, win_up, win_down,
    )
    stream, normed = pl.pallas_call(
        functools.partial(window_kernel, shape),
        out_shape=(
            jax.ShapeDtypeStruct((tokens, channels), f32),
            jax.ShapeDtypeStruct((tokens, channels), bf16),
        ),
        in_specs=[pl.BlockSpec(memory_space=pltpu.HBM)] * len(sources),
        out_specs=tuple(in_vmem(2)),
        scratch_shapes=[pltpu.VMEM(source.shape, source.dtype) for source in sources]
        + [
            pltpu.SemaphoreType.DMA((len(sources),)),
            pltpu.VMEM((channels // LANES, tokens, LANES), f32),
            pltpu.VMEM((breadth, rows, 3 * channels), bf16),
            pltpu.VMEM((breadth, rows, channels), bf16),
        ],
        compiler_params=pltpu.CompilerParams(vmem_limit_bytes=60 * 1024 * 1024),
    )(*sources)

    groups = lax.axis_size("member")
    blocks = [normed]
    bit = 1
    while bit * 2 < groups:
        bit *= 2
    far = [lax.ppermute(normed, "member", [(i, i ^ bit) for i in range(groups)])]
    partners = []
    while bit > 1:
        bit //= 2
        partners.append([(i, i ^ bit) for i in range(groups)])

    def spread(blocks):
        for partner in partners:
            blocks = blocks + [lax.ppermute(block, "member", partner) for block in blocks]
        return blocks

    near = spread([normed])
    part_shape = jax.ShapeDtypeStruct((breadth, rows, channels), f32)
    queries, *parts = pl.pallas_call(
        functools.partial(near_kernel, shape),
        out_shape=(jax.ShapeDtypeStruct((breadth, rows, channels), bf16),) + (part_shape,) * 3,
        in_specs=in_vmem(1 + len(near)),
        out_specs=tuple(in_vmem(4)),
        scratch_shapes=[pltpu.VMEM((breadth, rows * len(near), 2 * channels), bf16)],
        compiler_params=params,
    )(*near, mem_qkv)
    branch = offsets[1] - 1
    far[0], branch, queries, *parts = lax.optimization_barrier((far[0], branch, queries, *parts))
    far = spread(far)

    lat_count, lon_count = lax.axis_size("lat"), lax.axis_size("lon")
    lat_index = lax.axis_index("lat")
    down = [(i, i + 1) for i in range(lat_count - 1)]
    up = [(b, a) for a, b in down]
    lat_pairs = [down + up] if lat_count == 2 else [down, up]
    late, normed, *edges = pl.pallas_call(
        functools.partial(member_kernel, shape, lat_count),
        out_shape=(
            jax.ShapeDtypeStruct((tokens, channels), f32),
            jax.ShapeDtypeStruct((tokens, channels), bf16),
        )
        + (jax.ShapeDtypeStruct((edge_tokens, channels), bf16),) * len(lat_pairs),
        in_specs=in_vmem(7 + len(far)),
        out_specs=tuple(in_vmem(2 + len(lat_pairs))),
        scratch_shapes=[
            pltpu.VMEM((breadth, rows * len(far), 2 * channels), bf16),
            pltpu.VMEM((breadth, rows, channels), bf16),
        ],
        compiler_params=params,
    )(stream, queries, *parts, *far, mem_qkv, mem_out)

    ring = [(i, (i + 1) % lon_count) for i in range(lon_count)]
    back = [(b, a) for a, b in ring]

    def gather(amount, own, *edges):
        low = lax.ppermute(own[amount:], "lon", ring)
        high = lax.ppermute(own[:amount], "lon", back)

        def diagonal(block, lat_pairs, lon_pairs):
            pairs = [
                (a * lon_count + c, b * lon_count + d) for a, b in lat_pairs for c, d in lon_pairs
            ]
            return lax.ppermute(block, ("lat", "lon"), pairs)

        lines = members * WIN * amount
        low_corners = [diagonal(edge[lines:], pairs, ring) for edge, pairs in zip(edges, lat_pairs)]
        longer = amount
        if 2 * amount > breadth:
            longer = min(breadth, max(amount, 2 * (breadth - amount) + 1))
        some = members * WIN * longer
        high_corners = [diagonal(edge[:some], pairs, back) for edge, pairs in zip(edges, lat_pairs)]
        straight = [lax.ppermute(edge, "lat", pairs) for edge, pairs in zip(edges, lat_pairs)]
        if lat_count > 2:
            above = jnp.tile(jnp.arange(WIN, dtype=jnp.int32) >= offsets[0], breadth * members)[:, None]
            straight = [jnp.where(above, *straight)]
            low_corners = [jnp.where(above[lines:], *low_corners)]
            high_corners = [jnp.where(above[:some], *high_corners)]
        whole_shape = (members, breadth * height, channels)
        early = pl.pallas_call(
            functools.partial(early_kernel, shape, lat_count, amount),
            out_shape=(jax.ShapeDtypeStruct(whole_shape, bf16),)
            + (jax.ShapeDtypeStruct(whole_shape, f32),) * 3
            + (jax.ShapeDtypeStruct((breadth * height, 2 * breadth * WIN), f32),),
            in_specs=in_vmem(5),
            out_specs=tuple(in_vmem(5)),
            scratch_shapes=[
                pltpu.VMEM((breadth, rows, 3 * channels), bf16),
                pltpu.VMEM((breadth, rows, 2 * channels), bf16),
            ],
            compiler_params=params,
        )(offsets.reshape(1, -1), own.reshape(tokens, channels), high, low, shift_qkv)
        rim = high_corners[0], low_corners[0], straight[0]
        *rim, first = lax.optimization_barrier((*rim, early[0]))
        early = (first,) + tuple(early[1:])
        across, corner = pl.pallas_call(
            functools.partial(rim_kernel, shape, amount),
            out_shape=(jax.ShapeDtypeStruct((members, breadth * WIN, 2 * channels), bf16),) * 2,
            in_specs=in_vmem(4),
            out_specs=tuple(in_vmem(2)),
            compiler_params=params,
        )(*rim, shift_qkv)
        return early + (across, corner)

    *early, across, corner = lax.switch(
        branch,
        [functools.partial(gather, amount) for amount in range(1, WIN)],
        normed.reshape(breadth, rows, channels), *edges,
    )
    updated = pl.pallas_call(
        functools.partial(shift_kernel, shape),
        out_shape=jax.ShapeDtypeStruct((tokens, channels), bf16),
        in_specs=in_vmem(11),
        out_specs=pl.BlockSpec(memory_space=pltpu.VMEM),
        scratch_shapes=[
            pltpu.VMEM((breadth, rows, channels), bf16),
            pltpu.VMEM((channels // LANES, tokens, LANES), f32),
        ],
        compiler_params=params,
    )(late, *early, across, corner, shift_out, shift_up, shift_down)
    return updated.reshape(shape)


def solution(mesh):
    return jax.shard_map(
        per_device,
        mesh=mesh,
        in_specs=(P("member", "lat", "lon", None), P("lat", "lon")) + (P(),) * 12,
        out_specs=P("member", "lat", "lon", None),
        check_vma=False,
    )
```

```python
import functools

import jax
import jax.numpy as jnp
from jax import lax
from jax.experimental import pallas as pl
from jax.experimental.pallas import tpu as pltpu
from jax.sharding import PartitionSpec as P

HEADS = 4
WIN = 8
LANES = 128
EPSILON = 1e-05
MASKED = -1e30
VMEM_LIMIT = 40 * 1024 * 1024

f32 = jnp.float32
bf16 = jnp.bfloat16


def normalize(stream):
    average = jnp.mean(stream, axis=-1, keepdims=True)
    centered = stream - average
    spread = jnp.mean(centered * centered, axis=-1, keepdims=True)
    return (centered * lax.rsqrt(spread + EPSILON)).astype(bf16)


def dot(a, b):
    return jnp.dot(a, b, preferred_element_type=f32)


def head_lanes(channels):
    return lax.broadcasted_iota(jnp.int32, (1, channels), 1) // (channels // HEADS)


def partial_attention(query, key, value, bias):
    amount, channels = query.shape
    lanes = head_lanes(channels)
    scale = (channels // HEADS) ** (-0.5)
    stacked = jnp.concatenate(
        [query * jnp.where(lanes == head, scale, 0.0).astype(bf16) for head in range(HEADS)], axis=0
    )
    scores = lax.dot_general(stacked, key, (((1,), (1,)), ((), ())), preferred_element_type=f32)
    scores = scores.reshape(HEADS, amount, key.shape[0]) + bias[None]
    top = jnp.max(scores, axis=-1, keepdims=True)
    powers = jnp.exp(scores - top)
    total = jnp.sum(powers, axis=-1, keepdims=True)
    mixed = dot(powers.astype(bf16).reshape(HEADS * amount, key.shape[0]), value)

    def in_lanes(parts):
        result = parts[0]
        for head in range(1, HEADS):
            result = jnp.where(lanes == head, parts[head], result)
        return jnp.broadcast_to(result, (amount, channels))

    return in_lanes(mixed.reshape(HEADS, amount, channels)), in_lanes(top), in_lanes(total)


def joined_attention(one, two):
    top = jnp.maximum(one[1], two[1])
    first, second = jnp.exp(one[1] - top), jnp.exp(two[1] - top)
    return (first * one[0] + second * two[0]) / (first * one[2] + second * two[2])


def attend(query, key, value, bias):
    mixed, _, total = partial_attention(query, key, value, bias)
    return (mixed / total).astype(bf16)


def feed_forward(stream, up_ref, down_ref, chunk=256):
    normed = normalize(stream)
    total = stream
    for start in range(0, up_ref.shape[1], chunk):
        raw = dot(normed, up_ref[:, start : start + chunk])
        hidden = (0.5 * raw * (1.0 + lax.erf(raw * 0.5**0.5))).astype(bf16)
        total = total + dot(hidden, down_ref[start : start + chunk, :])
    return total


def window_kernel(
    shape, *refs
):
    members, height, breadth, channels = shape
    sources, refs = refs[:7], refs[7:]
    stream_ref, normed_ref, *places, semaphores, turned, held, attended = refs
    copies = [
        pltpu.make_async_copy(source, place, semaphores.at[index])
        for index, (source, place) in enumerate(zip(sources, places))
    ]
    for copy in copies[:4]:
        copy.start()
    fields_ref, land_ref, embed_ref, qkv_ref, out_ref, up_ref, down_ref = places
    rows = members * height
    for copy in copies[:3]:
        copy.wait()
    for copy in copies[4:]:
        copy.start()
    for part in range(channels // LANES):
        turned[part] = fields_ref[:, part * LANES : (part + 1) * LANES].astype(f32)
    same = lax.broadcasted_iota(jnp.int32, (1, height, height), 1) == lax.broadcasted_iota(
        jnp.int32, (1, height, height), 2
    )
    land = jnp.sum(
        jnp.where(same, land_ref[...].astype(f32)[:, None, :], 0.0), axis=-1, keepdims=True
    )
    columns = []
    for column in range(breadth):
        taken = jnp.concatenate(
            [turned[part, pl.ds(column, rows, stride=breadth), :] for part in range(channels // LANES)],
            axis=1,
        ).reshape(members, height, channels)
        columns.append((taken + (land[column] * embed_ref[...])[None]).reshape(rows, channels))
    stream = jnp.concatenate(columns, axis=0)
    normed = normalize(stream)
    copies[3].wait()
    held[...] = dot(normed, qkv_ref[...]).astype(bf16).reshape(breadth, rows, 3 * channels)
    tokens = breadth * height
    block = (lax.broadcasted_iota(jnp.int32, (tokens, tokens), 0) % height) // WIN
    other = (lax.broadcasted_iota(jnp.int32, (tokens, tokens), 1) % height) // WIN
    bias = jnp.where(block == other, 0.0, MASKED).astype(f32)
    for member in range(members):
        part = slice(member * height, (member + 1) * height)
        query, key, value = (
            held[:, part, i * channels : (i + 1) * channels].reshape(tokens, channels) for i in range(3)
        )
        attended[:, part, :] = attend(query, key, value, bias).reshape(breadth, height, channels)
    for copy in copies[4:]:
        copy.wait()
    stream = stream + dot(attended[...].reshape(breadth * rows, channels), out_ref[...])
    stream = feed_forward(stream, up_ref, down_ref)
    stream_ref[...] = stream
    normed_ref[...] = normalize(stream)


def member_pairs(shape, block_refs, qkv_ref, pairs):
    members, height, breadth, channels = shape
    rows = members * height
    for index, block_ref in enumerate(block_refs):
        pairs[:, index * rows : (index + 1) * rows, :] = (
            dot(block_ref[...], qkv_ref[:, channels:]).astype(bf16).reshape(breadth, rows, 2 * channels)
        )
    amount = pairs.shape[1]
    row = lax.broadcasted_iota(jnp.int32, (rows, amount), 0) % height
    other = lax.broadcasted_iota(jnp.int32, (rows, amount), 1) % height
    return jnp.where(row == other, 0.0, MASKED).astype(f32)


def near_kernel(shape, *refs):
    members, height, breadth, channels = shape
    *block_refs, qkv_ref, queries_ref, mixed_ref, top_ref, total_ref, pairs = refs
    rows = members * height
    queries_ref[...] = (
        dot(block_refs[0][...], qkv_ref[:, :channels]).astype(bf16).reshape(breadth, rows, channels)
    )
    bias = member_pairs(shape, block_refs, qkv_ref, pairs)
    for column in range(breadth):
        mixed_ref[column], top_ref[column], total_ref[column] = partial_attention(
            queries_ref[column], pairs[column, :, :channels], pairs[column, :, channels:], bias
        )


def member_kernel(shape, lat_count, stream_ref, queries_ref, mixed_ref, top_ref, total_ref, *refs):
    members, height, breadth, channels = shape
    sides = 1 if lat_count == 2 else 2
    *block_refs, qkv_ref, out_ref = refs[: -4 - sides]
    late_ref, normed_ref, *edge_refs = refs[-4 - sides : -2]
    pairs, attended = refs[-2:]
    rows = members * height
    bias = member_pairs(shape, block_refs, qkv_ref, pairs)
    for column in range(breadth):
        far = partial_attention(
            queries_ref[column], pairs[column, :, :channels], pairs[column, :, channels:], bias
        )
        near = mixed_ref[column], top_ref[column], total_ref[column]
        attended[column] = joined_attention(near, far).astype(bf16)
    stream = stream_ref[...] + dot(attended[...].reshape(breadth * rows, channels), out_ref[...])
    late_ref[...] = stream
    normed = normalize(stream)
    normed_ref[...] = normed
    lines = normed.astype(f32).reshape(breadth * members, height, channels)
    for edge_ref, edge in zip(edge_refs, lat_ends(lines, lat_count)):
        edge_ref[...] = edge.reshape(breadth * members * WIN, channels).astype(bf16)


def per_member(lines, members, breadth):
    lines = lines.reshape(breadth, members * WIN, lines.shape[-1])
    return [
        lines[:, member * WIN : (member + 1) * WIN].reshape(breadth * WIN, lines.shape[-1]).astype(bf16)
        for member in range(members)
    ]


def join_kernel(breadth, amount, first_ref, second_ref, side_ref):
    high_ref, low_ref = (first_ref, second_ref) if 2 * amount <= breadth else (second_ref, first_ref)
    side_ref[:amount] = high_ref[...]
    side_ref[amount:] = low_ref[...]


def lat_ends(lines, lat_count):
    top, bottom = lines[:, :WIN], lines[:, lines.shape[1] - WIN :]
    if lat_count == 2:
        return [jnp.where(lax.axis_index("lat") == 0, bottom, top)]
    return [bottom, top]


def lat_window(row, place_ref):
    return (row - place_ref[:, :1] + WIN) // WIN


def shifted_bias(shape, place_ref, key_lat, key_lon):
    members, height, breadth, channels = shape
    index = lax.broadcasted_iota(jnp.int32, (breadth * height, 1), 0)
    query_lon = jnp.where(index // height >= place_ref[:, 1:], 1, 0)
    query_tag = 2 * lat_window(index % height, place_ref) + query_lon
    return jnp.where(query_tag == 2 * key_lat + key_lon, 0.0, MASKED).astype(f32)


def early_kernel(
    shape, lat_count, place_ref, normed_ref, side_ref, qkv_ref,
    queries_ref, mixed_ref, top_ref, total_ref, late_bias_ref, held, beside,
):
    members, height, breadth, channels = shape
    rows, tokens = members * height, breadth * height
    held[...] = dot(normed_ref[...], qkv_ref[...]).astype(bf16).reshape(breadth, rows, 3 * channels)
    beside[...] = dot(side_ref[...], qkv_ref[:, channels:]).astype(bf16).reshape(
        breadth, rows, 2 * channels
    )
    index = lax.broadcasted_iota(jnp.int32, (1, 2 * tokens), 1)
    mixed, local = index // tokens, index % tokens
    key_lon = jnp.where(local // height >= place_ref[:, 1:], 1 - mixed, mixed)
    bias = shifted_bias(shape, place_ref, lat_window(local % height, place_ref), key_lon)
    for member in range(members):
        part = slice(member * height, (member + 1) * height)
        query = held[:, part, :channels].reshape(tokens, channels)
        queries_ref[member] = query
        key, value = (
            jnp.concatenate(
                [
                    held[:, part, (i + 1) * channels : (i + 2) * channels].reshape(tokens, channels),
                    beside[:, part, i * channels : (i + 1) * channels].reshape(tokens, channels),
                ],
                axis=0,
            )
            for i in range(2)
        )
        mixed_ref[member], top_ref[member], total_ref[member] = partial_attention(query, key, value, bias)

    edge_tokens = breadth * WIN
    first = jnp.where(lax.axis_index("lat") == 0, 1, 0)
    last = jnp.where(lax.axis_index("lat") == lat_count - 1, 1, 0)
    index = lax.broadcasted_iota(jnp.int32, (1, 2 * edge_tokens), 1)
    mixed, local = index // edge_tokens, index % edge_tokens
    key_lat = jnp.where(local % WIN >= place_ref[:, :1], -1000 * first, height // WIN - 1000 * last)
    key_lon = jnp.where(local // WIN >= place_ref[:, 1:], 1 - mixed, mixed)
    late_bias_ref[...] = shifted_bias(shape, place_ref, key_lat, key_lon)


def rim_kernel(shape, amount, high_ref, low_ref, edge_ref, qkv_ref, across_ref, corner_ref):
    members, height, breadth, channels = shape
    edge = per_member(dot(edge_ref[...], qkv_ref[:, channels:]), members, breadth)
    high, low = (dot(ref[...], qkv_ref[:, channels:]) for ref in (high_ref, low_ref))
    sides = [high[: members * WIN * amount], low]
    corner = per_member(jnp.concatenate(sides, axis=0), members, breadth)
    for member in range(members):
        across_ref[member] = edge[member]
        corner_ref[member] = corner[member]


def shift_kernel(
    shape, stream_ref, queries_ref, mixed_ref, top_ref, total_ref, bias_ref, across, corner, out_ref, up_ref,
    down_ref, updated_ref, attended, turned,
):
    members, height, breadth, channels = shape
    rows = members * height
    bias = bias_ref[...]
    for member in range(members):
        key, value = (
            jnp.concatenate(
                [block[member, :, i * channels : (i + 1) * channels] for block in (across, corner)], axis=0
            )
            for i in range(2)
        )
        late = partial_attention(queries_ref[member], key, value, bias)
        early = mixed_ref[member], top_ref[member], total_ref[member]
        attended[:, member * height : (member + 1) * height, :] = (
            joined_attention(early, late).astype(bf16).reshape(breadth, height, channels)
        )
    stream = stream_ref[...] + dot(attended[...].reshape(breadth * rows, channels), out_ref[...])
    stream = feed_forward(stream, up_ref, down_ref)
    for column in range(breadth):
        for part in range(channels // LANES):
            turned[part, pl.ds(column, rows, stride=breadth), :] = stream[
                column * rows : (column + 1) * rows, part * LANES : (part + 1) * LANES
            ]
    for part in range(channels // LANES):
        updated_ref[:, part * LANES : (part + 1) * LANES] = turned[part].astype(bf16)


def in_vmem(count):
    return [pl.BlockSpec(memory_space=pltpu.VMEM)] * count


def per_device(
    fields, land_mask, offsets, land_embed, win_qkv, win_out, win_up, win_down, mem_qkv, mem_out,
    shift_qkv, shift_out, shift_up, shift_down,
):
    shape = fields.shape
    members, height, breadth, channels = shape
    rows, tokens = members * height, members * height * breadth
    edge_tokens = members * WIN * breadth
    params = pltpu.CompilerParams(vmem_limit_bytes=VMEM_LIMIT)
    sources = (
        fields.reshape(tokens, channels), land_mask.T, land_embed.reshape(1, channels),
        win_qkv, win_out, win_up, win_down,
    )
    stream, normed = pl.pallas_call(
        functools.partial(window_kernel, shape),
        out_shape=(
            jax.ShapeDtypeStruct((tokens, channels), f32),
            jax.ShapeDtypeStruct((tokens, channels), bf16),
        ),
        in_specs=[pl.BlockSpec(memory_space=pltpu.HBM)] * len(sources),
        out_specs=tuple(in_vmem(2)),
        scratch_shapes=[pltpu.VMEM(source.shape, source.dtype) for source in sources]
        + [
            pltpu.SemaphoreType.DMA((len(sources),)),
            pltpu.VMEM((channels // LANES, tokens, LANES), f32),
            pltpu.VMEM((breadth, rows, 3 * channels), bf16),
            pltpu.VMEM((breadth, rows, channels), bf16),
        ],
        compiler_params=pltpu.CompilerParams(vmem_limit_bytes=60 * 1024 * 1024),
    )(*sources)

    groups = lax.axis_size("member")
    blocks = [normed]
    bit = 1
    while bit * 2 < groups:
        bit *= 2
    far = [lax.ppermute(normed, "member", [(i, i ^ bit) for i in range(groups)])]
    partners = []
    while bit > 1:
        bit //= 2
        partners.append([(i, i ^ bit) for i in range(groups)])

    def spread(blocks):
        for partner in partners:
            blocks = blocks + [lax.ppermute(block, "member", partner) for block in blocks]
        return blocks

    near = spread([normed])
    part_shape = jax.ShapeDtypeStruct((breadth, rows, channels), f32)
    queries, *parts = pl.pallas_call(
        functools.partial(near_kernel, shape),
        out_shape=(jax.ShapeDtypeStruct((breadth, rows, channels), bf16),) + (part_shape,) * 3,
        in_specs=in_vmem(1 + len(near)),
        out_specs=tuple(in_vmem(4)),
        scratch_shapes=[pltpu.VMEM((breadth, rows * len(near), 2 * channels), bf16)],
        compiler_params=params,
    )(*near, mem_qkv)
    branch = offsets[1] - 1
    far[0], branch, queries, *parts = lax.optimization_barrier((far[0], branch, queries, *parts))
    far = spread(far)

    lat_count, lon_count = lax.axis_size("lat"), lax.axis_size("lon")
    lat_index = lax.axis_index("lat")
    down = [(i, i + 1) for i in range(lat_count - 1)]
    up = [(b, a) for a, b in down]
    lat_pairs = [down + up] if lat_count == 2 else [down, up]
    late, normed, *edges = pl.pallas_call(
        functools.partial(member_kernel, shape, lat_count),
        out_shape=(
            jax.ShapeDtypeStruct((tokens, channels), f32),
            jax.ShapeDtypeStruct((tokens, channels), bf16),
        )
        + (jax.ShapeDtypeStruct((edge_tokens, channels), bf16),) * len(lat_pairs),
        in_specs=in_vmem(7 + len(far)),
        out_specs=tuple(in_vmem(2 + len(lat_pairs))),
        scratch_shapes=[
            pltpu.VMEM((breadth, rows * len(far), 2 * channels), bf16),
            pltpu.VMEM((breadth, rows, channels), bf16),
        ],
        compiler_params=params,
    )(stream, queries, *parts, *far, mem_qkv, mem_out)

    ring = [(i, (i + 1) % lon_count) for i in range(lon_count)]
    back = [(b, a) for a, b in ring]

    def gather(amount, own, *edges):
        low = lax.ppermute(own[amount:], "lon", ring)
        high = lax.ppermute(own[:amount], "lon", back)

        def diagonal(block, lat_pairs, lon_pairs):
            pairs = [
                (a * lon_count + c, b * lon_count + d) for a, b in lat_pairs for c, d in lon_pairs
            ]
            return lax.ppermute(block, ("lat", "lon"), pairs)

        lines = members * WIN * amount
        low_corners = [diagonal(edge[lines:], pairs, ring) for edge, pairs in zip(edges, lat_pairs)]
        longer = amount
        if 2 * amount > breadth:
            longer = min(breadth, max(amount, 2 * (breadth - amount) + 1))
        some = members * WIN * longer
        high_corners = [diagonal(edge[:some], pairs, back) for edge, pairs in zip(edges, lat_pairs)]
        straight = [lax.ppermute(edge, "lat", pairs) for edge, pairs in zip(edges, lat_pairs)]
        if lat_count > 2:
            above = jnp.tile(jnp.arange(WIN, dtype=jnp.int32) >= offsets[0], breadth * members)[:, None]
            straight = [jnp.where(above, *straight)]
            low_corners = [jnp.where(above[lines:], *low_corners)]
            high_corners = [jnp.where(above[:some], *high_corners)]
        side = pl.pallas_call(
            functools.partial(join_kernel, breadth, amount),
            out_shape=jax.ShapeDtypeStruct((breadth, rows, channels), bf16),
            in_specs=in_vmem(2),
            out_specs=in_vmem(1)[0],
            compiler_params=params,
        )(*((high, low) if 2 * amount <= breadth else (low, high)))
        whole_shape = (members, breadth * height, channels)
        early = pl.pallas_call(
            functools.partial(early_kernel, shape, lat_count),
            out_shape=(jax.ShapeDtypeStruct(whole_shape, bf16),)
            + (jax.ShapeDtypeStruct(whole_shape, f32),) * 3
            + (jax.ShapeDtypeStruct((breadth * height, 2 * breadth * WIN), f32),),
            in_specs=in_vmem(4),
            out_specs=tuple(in_vmem(5)),
            scratch_shapes=[
                pltpu.VMEM((breadth, rows, 3 * channels), bf16),
                pltpu.VMEM((breadth, rows, 2 * channels), bf16),
            ],
            compiler_params=params,
        )(offsets.reshape(1, -1), own.reshape(tokens, channels), side.reshape(tokens, channels), shift_qkv)
        rim = high_corners[0], low_corners[0], straight[0]
        *rim, first = lax.optimization_barrier((*rim, early[0]))
        early = (first,) + tuple(early[1:])
        across, corner = pl.pallas_call(
            functools.partial(rim_kernel, shape, amount),
            out_shape=(jax.ShapeDtypeStruct((members, breadth * WIN, 2 * channels), bf16),) * 2,
            in_specs=in_vmem(4),
            out_specs=tuple(in_vmem(2)),
            compiler_params=params,
        )(*rim, shift_qkv)
        return early + (across, corner)

    *early, across, corner = lax.switch(
        branch,
        [functools.partial(gather, amount) for amount in range(1, WIN)],
        normed.reshape(breadth, rows, channels), *edges,
    )
    updated = pl.pallas_call(
        functools.partial(shift_kernel, shape),
        out_shape=jax.ShapeDtypeStruct((tokens, channels), bf16),
        in_specs=in_vmem(11),
        out_specs=pl.BlockSpec(memory_space=pltpu.VMEM),
        scratch_shapes=[
            pltpu.VMEM((breadth, rows, channels), bf16),
            pltpu.VMEM((channels // LANES, tokens, LANES), f32),
        ],
        compiler_params=params,
    )(late, *early, across, corner, shift_out, shift_up, shift_down)
    return updated.reshape(shape)


def solution(mesh):
    return jax.shard_map(
        per_device,
        mesh=mesh,
        in_specs=(P("member", "lat", "lon", None), P("lat", "lon")) + (P(),) * 12,
        out_specs=P("member", "lat", "lon", None),
        check_vma=False,
    )
```
